32 devices in a mesh: groups: 2 (over x), mesh: 16 (over z, y, core).
Axes of the slice: x: 2, y: 2, z: 4, core: 2. Of those that a mesh axis runs over, the one named last changes fastest.
Arguments:
- water_depth: float32 [768, 10, 640], P(('groups', 'mesh')), parts along dimension 0, may hold values from 1 to 3
- momentum: float32 [768, 2, 10, 640], P(('groups', 'mesh')), parts along dimension 0, may hold values from -3 to 3
- metric: float32 [768, 4, 64], P(('groups', 'mesh')), parts along dimension 0, may hold values from -2 to 2
- face_scale: float32 [768, 192], P(('groups', 'mesh')), parts along dimension 0, may hold values from 0.5 to 2
- face_angle: float32 [768, 192], P(('groups', 'mesh')), parts along dimension 0, may hold values from -3.140625 to 3.140625
- face_map: int32 [768, 192], P(('groups', 'mesh')), parts along dimension 0, may hold values from 0 to 4735, as said below
- rim_faces: int32 [32, 128], P(('groups', 'mesh')), parts along dimension 0, may hold values from 0 to 4607, as said below
- wet_blocks: int32 [768], P(('groups', 'mesh')), parts along dimension 0, may hold values from 0 to 1, as said below
- breach: int32 [768, 10], P(('groups', 'mesh')), parts along dimension 0, may hold values from 0 to 3
- block_plan: int32 [768], P('groups'), parts along dimension 0, may hold values from 0 to 383, as said below
Outputs:
- depth_out: float32 [768, 10, 640], P(('groups', 'mesh')), parts along dimension 0
- momentum_out: float32 [768, 2, 10, 640], P(('groups', 'mesh')), parts along dimension 0
The draws below stay inside these ranges and needn't reach their ends.
There are 2 independent parts, one for each index of `groups`. The reference program is written for one: setup_inputs(seed, part) draws one part's arguments, and reference() takes and returns one part's arrays. A program takes and returns all parts, laid end to end along the dimension named above; each array names one. Nothing has to cross between parts.
Inputs may be any that keep to these rules, and one draw needn't show every extreme that they name: `face_map`: per mesh index d, the values of its rows name faces as in the reference program: a local face number, where the pairing of local faces is symmetric, or an entry of the neighbouring index's rim list. The rim entries pair in order: entry i of index d's second half of rim_faces with entry i of index d + 1's first half. No face of the first index names a previous index, none of the last a next one. `rim_faces`: each row holds 128 distinct local face numbers. `wet_blocks`: every block of mesh index 0 is 1; the chance of a 1 falls along the mesh axis. `block_plan`: A permutation of the block slots. Each mesh index hands exactly 8 of its blocks to other indices, each to a different index, and receives exactly 8, each from a different index, into the slots it vacates; the other blocks stay.
All inputs are finite; a program needn't handle non-finite values.
Results may differ from the reference program's by a relative error of at most 0.000059.
Values sent between devices are 32-bit elements; how exact they have to be, the bound alone decides.
A program may use at most 192 MiB of HBM per device.

```python
import math
import jax
import jax.numpy as jnp
import numpy as np
from jax import lax

S = 10
NP = 10
BLK = 64
BLK_DEV = 24
MOVE_DEV = 8
RIM = 64
NBLK = 384
N_MESH = 16


def topology(key):
    parts_count = NBLK // BLK_DEV
    faces_dev = 3 * BLK * BLK_DEV

    def one_device(device):
        shuffled = jax.random.permutation(jax.random.fold_in(key, device), faces_dev).astype(jnp.int32)
        left_rim = shuffled[:RIM]
        right_rim = shuffled[RIM:2 * RIM]
        wall_faces = shuffled[2 * RIM:3 * RIM]
        remaining = shuffled[3 * RIM:]
        first_half = remaining[0::2]
        second_half = remaining[1::2]
        neighbours = jnp.zeros((faces_dev,), jnp.int32)
        neighbours = neighbours.at[first_half].set(second_half).at[second_half].set(first_half).at[wall_faces].set(wall_faces)
        positions = jnp.arange(RIM, dtype=jnp.int32)
        neighbours = neighbours.at[left_rim].set(jnp.where(device == 0, left_rim, faces_dev + positions))
        neighbours = neighbours.at[right_rim].set(jnp.where(device == parts_count - 1, right_rim, faces_dev + RIM + positions))
        return (neighbours, jnp.concatenate([left_rim, right_rim]))
    neighbours, rim_lists = jax.vmap(one_device)(jnp.arange(parts_count, dtype=jnp.int32))
    return (neighbours.reshape(NBLK, 3 * BLK), rim_lists)


def draw_face_map(key, part):
    return topology(jax.random.fold_in(key, 11))[0]


def draw_rim_faces(key, part):
    return topology(jax.random.fold_in(key, 11))[1]


def draw_wet_blocks(key, part):
    parts_count = NBLK // BLK_DEV
    levels = jax.random.randint(key, (NBLK,), 0, parts_count)
    owners = jnp.arange(NBLK, dtype=jnp.int32) // BLK_DEV
    return (levels >= owners).astype(jnp.int32)


def draw_block_plan(key, part):
    parts_count = NBLK // BLK_DEV
    base_key = jax.random.fold_in(key, 23)
    offsets = 1 + jax.random.permutation(jax.random.fold_in(base_key, 1), parts_count - 1)[:MOVE_DEV].astype(jnp.int32)
    labels = jax.random.permutation(jax.random.fold_in(base_key, 2), parts_count).astype(jnp.int32)
    devices = jnp.arange(parts_count, dtype=jnp.int32)
    inverse = jnp.zeros((parts_count,), jnp.int32).at[labels].set(devices)
    shuffles = jax.vmap(lambda device: jax.random.permutation(jax.random.fold_in(jax.random.fold_in(base_key, 3), device), BLK_DEV))(devices).astype(jnp.int32)
    arrivals = jax.vmap(lambda device: jax.random.permutation(jax.random.fold_in(jax.random.fold_in(base_key, 4), device), MOVE_DEV))(devices).astype(jnp.int32)
    targets = labels[(inverse[:, None] + offsets[None, :]) % parts_count]
    sources = devices[:, None] * BLK_DEV + shuffles[:, :MOVE_DEV]
    moving_index = jnp.arange(MOVE_DEV, dtype=jnp.int32)[None, :]
    dest_slot = shuffles[targets, arrivals[targets, moving_index]]
    destinations = targets * BLK_DEV + dest_slot
    return jnp.arange(NBLK, dtype=jnp.int32).at[sources.reshape(-1)].set(destinations.reshape(-1).astype(jnp.int32))


def with_ends(values, rng, low, top_value):
    dims = values.shape
    place = [jax.random.randint(jax.random.fold_in(rng, axis), (), 0, dims[axis]) for axis in range(len(dims))]
    values = values.at[tuple(place)].set(low)
    longest = dims.index(max(dims))
    place[longest] = (place[longest] + 1) % dims[longest]
    return values.at[tuple(place)].set(top_value)


def steps_of(key, shape, pieces, low, high):
    gain, own = 1.0, jax.random.fold_in(key, 6)
    for dim, blocks in pieces:
        draws = jnp.exp(jax.random.uniform(jax.random.fold_in(own, dim), (blocks,), jnp.float32, low / len(pieces), high / len(pieces)))
        gain = gain * jnp.repeat(draws, shape[dim] // blocks).reshape([-1 if axis == dim else 1 for axis in range(len(shape))])
    return gain


def centred(own_key, shape, width, bound, pieces=(), held_as=jnp.bfloat16):
    entries = jax.random.normal(own_key, shape, jnp.float32) * width
    if len(pieces) > 0:
        entries = steps_of(own_key, shape, pieces, -0.22, 0.18) * entries
    return jnp.clip(entries, min=-bound, max=bound).astype(held_as)


def setup_inputs(seed: int = 0, part: int = 0) -> dict:
    seeds = jax.random.split(jax.random.key(seed), 11)
    own_keys = jax.random.split(jax.random.fold_in(seeds[10], part), 11)
    return {
        "water_depth": jnp.clip(1.0 + 2.0 * jax.random.uniform(own_keys[0], (NBLK, S, NP * BLK), jnp.float32) ** steps_of(own_keys[0], (NBLK, S, NP * BLK), ((0, 16),), -0.2, 0.2), 1.0, 3.0),
        "momentum": centred(own_keys[1], (NBLK, 2, S, NP * BLK), 0.5, 3.0, ((0, 16),), jnp.float32),
        "metric": centred(own_keys[2], (NBLK, 4, BLK), 0.5, 2.0, ((0, 16),), jnp.float32),
        "face_scale": jnp.clip(jnp.exp(math.log(2.0) - 1.3862944 * jax.random.uniform(own_keys[3], (NBLK, 3 * BLK), jnp.float32) ** steps_of(own_keys[3], (NBLK, 3 * BLK), ((0, 16),), -0.2, 0.2)), 0.5, 2.0),
        "face_angle": jnp.clip(jax.random.uniform(own_keys[4], (NBLK, 3 * BLK), jnp.float32, -3.140625, 3.140625), -3.140625, 3.140625),
        "face_map": draw_face_map(jax.random.fold_in(jax.random.fold_in(seeds[10], part), 71), part),
        "rim_faces": draw_rim_faces(jax.random.fold_in(jax.random.fold_in(seeds[10], part), 71), part),
        "wet_blocks": draw_wet_blocks(jax.random.fold_in(jax.random.fold_in(seeds[10], part), 71), part),
        "breach": with_ends(jax.random.randint(own_keys[8], (NBLK, S), 0, 4), jax.random.fold_in(own_keys[8], 1), 0, 3).astype(jnp.int32),
        "block_plan": draw_block_plan(jax.random.fold_in(jax.random.fold_in(seeds[10], part), 71), part),
    }


time_step = 0.01
gravity = 1.0
breach_rate = 5.0

def gauss_solve(matrix, right):
    dimension = matrix.shape[0]
    augmented = np.concatenate([np.array(matrix) * 1.0, np.array(right) * 1.0], axis=1)
    for pivot_col in range(dimension):
        largest = pivot_col + int(np.argmax(np.abs(augmented[pivot_col:, pivot_col])))
        swapped = augmented[[largest, pivot_col]]
        augmented[[pivot_col, largest]] = swapped
        augmented[pivot_col] = augmented[pivot_col] / augmented[pivot_col, pivot_col]
        for row_id in range(dimension):
            if row_id != pivot_col:
                augmented[row_id] = augmented[row_id] - augmented[row_id, pivot_col] * augmented[pivot_col]
    return augmented[:, dimension:]

def node_tables():
    points = np.array([(across / 3.0, upward / 3.0) for upward in range(4) for across in range(4 - upward)])
    powers = [(power_r, power_s) for power_r in range(4) for power_s in range(4 - power_r)]
    vander = np.zeros((10, 10))
    grad_r = np.zeros((10, 10))
    grad_s = np.zeros((10, 10))
    mono_mass = np.zeros((10, 10))
    for column, (power_r, power_s) in enumerate(powers):
        vander[:, column] = points[:, 0] ** power_r * points[:, 1] ** power_s
        if power_r > 0:
            grad_r[:, column] = power_r * points[:, 0] ** (power_r - 1) * points[:, 1] ** power_s
        if power_s > 0:
            grad_s[:, column] = power_s * points[:, 0] ** power_r * points[:, 1] ** (power_s - 1)
        for second_column, (other_r, other_s) in enumerate(powers):
            mono_mass[column, second_column] = math.factorial(power_r + other_r) * math.factorial(power_s + other_s) / math.factorial(power_r + other_r + power_s + other_s + 2)
    inverse = gauss_solve(vander, np.eye(10))
    mass_matrix = inverse.T @ mono_mass @ inverse
    line_points = np.arange(4) / 3.0
    line_vander = line_points[:, None] ** np.arange(4)[None, :]
    hilbert = 1.0 / (np.arange(4)[:, None] + np.arange(4)[None, :] + 1.0)
    line_inverse = gauss_solve(line_vander, np.eye(4))
    edge_mass = line_inverse.T @ hilbert @ line_inverse
    face_nodes = np.array([[0, 1, 2, 3], [3, 6, 8, 9], [9, 7, 4, 0]])
    edge_embed = np.zeros((10, 12))
    for face_id in range(3):
        for node_id in range(4):
            edge_embed[face_nodes[face_id, node_id], 4 * face_id:4 * face_id + 4] += edge_mass[node_id]
    lifting = gauss_solve(mass_matrix, edge_embed).reshape(10, 3, 4)
    return (jnp.asarray(grad_r @ inverse, jnp.float32), jnp.asarray(grad_s @ inverse, jnp.float32), jnp.asarray(lifting, jnp.float32), face_nodes.reshape(-1))

def normal_flux(height, flow_x, flow_y, normal_x, normal_y):
    normal_speed = (flow_x * normal_x + flow_y * normal_y) / height
    pressure = 0.5 * gravity * height * height
    fluxes = jnp.stack([flow_x * normal_x + flow_y * normal_y, flow_x * normal_speed + pressure * normal_x, flow_y * normal_speed + pressure * normal_y])
    return (fluxes, jnp.abs(normal_speed) + jnp.sqrt(gravity * height))

def flux_jumps(interior, exterior, wall_faces, normal_x, normal_y, face_scale):
    normal_flow = interior[1] * normal_x + interior[2] * normal_y
    mirrored = jnp.stack([interior[0], interior[1] - 2.0 * normal_flow * normal_x, interior[2] - 2.0 * normal_flow * normal_y])
    exterior = jnp.where(wall_faces, mirrored, exterior)
    inner_flux, inner_speed = normal_flux(interior[0], interior[1], interior[2], normal_x, normal_y)
    outer_flux, outer_speed = normal_flux(exterior[0], exterior[1], exterior[2], normal_x, normal_y)
    wave_speed = jnp.maximum(inner_speed, outer_speed)
    return face_scale * (0.5 * (inner_flux - outer_flux) + 0.5 * wave_speed * (exterior - interior))

def face_traces(fields, face_order):
    blocks, components, members, node_count, elements = fields.shape
    picked = fields[:, :, :, face_order, :].reshape(blocks, components, members, 3, 4, elements)
    return picked.transpose(1, 2, 4, 0, 3, 5).reshape(components, members, 4, blocks * 3 * elements)

def apply_matrix(matrix, values):
    return jnp.einsum('nm,bvsme->bvsne', matrix, values, precision=lax.Precision.HIGHEST)

def advance(fields, face_jumps, metric, wet_blocks, breach, tables):
    deriv_r, deriv_s, lifting, face_order = tables
    blocks, components, members, node_count, elements = fields.shape
    shaped = face_jumps.reshape(components, members, 4, blocks, 3, elements)
    lifted = jnp.einsum('nfj,vsjbfe->bvsne', lifting, shaped, precision=lax.Precision.HIGHEST)
    height = fields[:, 0]
    flow_x = fields[:, 1]
    flow_y = fields[:, 2]
    pressure = 0.5 * gravity * height * height
    speed_x = flow_x / height
    speed_y = flow_y / height
    flux_f = jnp.stack([flow_x, flow_x * speed_x + pressure, flow_y * speed_x], axis=1)
    flux_g = jnp.stack([flow_y, flow_x * speed_y, flow_y * speed_y + pressure], axis=1)
    factors = metric[:, :, None, None, None, :]
    divergence = factors[:, 0] * apply_matrix(deriv_r, flux_f) + factors[:, 1] * apply_matrix(deriv_s, flux_f) + factors[:, 2] * apply_matrix(deriv_r, flux_g) + factors[:, 3] * apply_matrix(deriv_s, flux_g)
    inflow = breach_rate * breach.astype(jnp.float32)[:, None, :, None, None] * (jnp.arange(3) == 0).astype(jnp.float32)[None, :, None, None, None]
    tendency = lifted - divergence + inflow
    return fields + time_step * wet_blocks.astype(jnp.float32)[:, None, None, None, None] * tendency

def reference(water_depth, momentum, metric, face_scale, face_angle, face_map, rim_faces, wet_blocks, breach, block_plan):
    tables = node_tables()
    node_count = tables[0].shape[0]
    blocks, members, node_cells = water_depth.shape
    elements = node_cells // node_count
    fields = jnp.concatenate([water_depth[:, None], momentum], axis=1).reshape(blocks, 3, members, node_count, elements)
    traces = face_traces(fields, tables[3])
    faces_dev = 3 * elements * BLK_DEV
    face_links = face_map.reshape(N_MESH, faces_dev).astype(jnp.int32)
    device = jnp.arange(N_MESH, dtype=jnp.int32)[:, None]
    before_dev = jnp.clip(device - 1, 0, N_MESH - 1)
    after_dev = jnp.clip(device + 1, 0, N_MESH - 1)
    from_before = jnp.take_along_axis(rim_faces[before_dev[:, 0], RIM:], jnp.clip(face_links - faces_dev, 0, RIM - 1), axis=1)
    from_after = jnp.take_along_axis(rim_faces[after_dev[:, 0], :RIM], jnp.clip(face_links - faces_dev - RIM, 0, RIM - 1), axis=1)
    partner = jnp.where(face_links < faces_dev, device * faces_dev + face_links, jnp.where(face_links < faces_dev + RIM, before_dev * faces_dev + from_before, after_dev * faces_dev + from_after)).astype(jnp.int32)
    wall_faces = (face_links == jnp.arange(faces_dev, dtype=jnp.int32)[None, :]).reshape(-1)
    exterior = jnp.take(traces, partner.reshape(-1), axis=3)[:, :, ::-1]
    angles = face_angle.reshape(-1)
    face_jumps = flux_jumps(traces, exterior, wall_faces, jnp.cos(angles), jnp.sin(angles), face_scale.reshape(-1))
    advanced = advance(fields, face_jumps, metric, wet_blocks, breach, tables)
    new_depth = advanced[:, 0].reshape(blocks, members, node_cells)
    new_flow = advanced[:, 1:].reshape(blocks, 2, members, node_cells)
    return (jnp.zeros_like(new_depth).at[block_plan].set(new_depth), jnp.zeros_like(new_flow).at[block_plan].set(new_flow))
```

```python
import math

import jax
import jax.numpy as jnp
import numpy as np
import ml_dtypes
from jax import lax
from jax.experimental import pallas as pl
from jax.experimental.pallas import tpu as pltpu
from jax.sharding import PartitionSpec as P

time_step = 0.01
gravity = 1.0
breach_rate = 5.0


SMEM = pl.BlockSpec(memory_space=pltpu.SMEM)
VMEM = pl.BlockSpec(memory_space=pltpu.VMEM)
ANY = pl.BlockSpec(memory_space=pl.ANY)
faces, face_points = 3, 4


def gauss_solve(matrix, right):
    dimension = matrix.shape[0]
    augmented = np.concatenate([np.array(matrix) * 1.0, np.array(right) * 1.0], axis=1)
    for pivot_col in range(dimension):
        largest = pivot_col + int(np.argmax(np.abs(augmented[pivot_col:, pivot_col])))
        swapped = augmented[[largest, pivot_col]]
        augmented[[pivot_col, largest]] = swapped
        augmented[pivot_col] = augmented[pivot_col] / augmented[pivot_col, pivot_col]
        for row_id in range(dimension):
            if row_id != pivot_col:
                augmented[row_id] = (
                    augmented[row_id] - augmented[row_id, pivot_col] * augmented[pivot_col]
                )
    return augmented[:, dimension:]


def node_tables():
    points = np.array(
        [(across / 3.0, upward / 3.0) for upward in range(4) for across in range(4 - upward)]
    )
    powers = [(power_r, power_s) for power_r in range(4) for power_s in range(4 - power_r)]
    vander = np.zeros((10, 10))
    grad_r = np.zeros((10, 10))
    grad_s = np.zeros((10, 10))
    mono_mass = np.zeros((10, 10))
    for column, (power_r, power_s) in enumerate(powers):
        vander[:, column] = points[:, 0] ** power_r * points[:, 1] ** power_s
        if power_r > 0:
            grad_r[:, column] = power_r * points[:, 0] ** (power_r - 1) * points[:, 1] ** power_s
        if power_s > 0:
            grad_s[:, column] = power_s * points[:, 0] ** power_r * points[:, 1] ** (power_s - 1)
        for second_column, (other_r, other_s) in enumerate(powers):
            mono_mass[column, second_column] = (
                math.factorial(power_r + other_r)
                * math.factorial(power_s + other_s)
                / math.factorial(power_r + other_r + power_s + other_s + 2)
            )
    inverse = gauss_solve(vander, np.eye(10))
    mass_matrix = inverse.T @ mono_mass @ inverse
    line_points = np.arange(4) / 3.0
    line_vander = line_points[:, None] ** np.arange(4)[None, :]
    hilbert = 1.0 / (np.arange(4)[:, None] + np.arange(4)[None, :] + 1.0)
    line_inverse = gauss_solve(line_vander, np.eye(4))
    edge_mass = line_inverse.T @ hilbert @ line_inverse
    face_nodes = np.array([[0, 1, 2, 3], [3, 6, 8, 9], [9, 7, 4, 0]])
    edge_embed = np.zeros((10, 12))
    for face_id in range(3):
        for node_id in range(4):
            edge_embed[face_nodes[face_id, node_id], 4 * face_id : 4 * face_id + 4] += edge_mass[
                node_id
            ]
    lifting = gauss_solve(mass_matrix, edge_embed).reshape(10, 3, 4)
    return (
        np.asarray(grad_r @ inverse, np.float32),
        np.asarray(grad_s @ inverse, np.float32),
        np.asarray(lifting, np.float32),
        face_nodes,
    )


def round_up(count, step):
    return -(-count // step) * step


def combined_matrix(members, rows, node_count):
    deriv_r, deriv_s, lifting, _ = node_tables()
    full = members // 8 * 8
    rest = members - full
    face_rows = face_points * members
    columns = 2 * rows + round_up(faces * face_rows, 16)

    def place(point, member, points):
        if member < full:
            return point * full + member
        return points * full + point * rest + member - full

    table = np.zeros((rows, columns), np.float32)
    for member in range(members):
        for node in range(node_count):
            row = place(node, member, node_count)
            for other in range(node_count):
                column = place(other, member, node_count)
                table[row, column] = -deriv_r[node, other]
                table[row, rows + column] = -deriv_s[node, other]
            for face in range(faces):
                for point in range(face_points):
                    column = 2 * rows + face * face_rows + place(point, member, face_points)
                    table[row, column] = lifting[node, face, point]
    high = table.astype(ml_dtypes.bfloat16)
    low = (table - high.astype(np.float32)).astype(ml_dtypes.bfloat16)
    return high, low


def lanes_low(shape, elements):
    return lax.broadcasted_iota(jnp.int32, shape, len(shape) - 1) < elements


def stack_face(fields_ref, pair, comp, nodes, members, node_count, out_ref, start):
    full = members // 8 * 8
    rest = members - full
    for point, node in enumerate(nodes):
        out_ref[start + point * full : start + (point + 1) * full, :] = fields_ref[
            pair, comp, node * full : (node + 1) * full, :
        ]
    base = node_count * full
    tail = start + len(nodes) * full
    for point, node in enumerate(nodes):
        out_ref[tail + point * rest : tail + (point + 1) * rest, :] = fields_ref[
            pair, comp, base + node * rest : base + (node + 1) * rest, :
        ]


def layout_kernel(
    face_nodes, node_count, depth_ref, flow_ref, rim_ref, fields_ref, table_ref, edge_ref, stack_ref
):
    blocks, members, node_cells = depth_ref.shape
    elements = node_cells // node_count
    lanes = 2 * elements
    full = members // 8 * 8
    rest = members - full
    used = node_count * members
    rows = fields_ref.shape[2]
    face_rows = face_points * members
    stack_ref[...] = jnp.zeros_like(stack_ref)

    def one_pair(pair, carry):
        for comp in range(3):
            fields_ref[pair, comp, used:rows, :] = jnp.ones((rows - used, lanes), jnp.float32)
            for half in range(node_count // 2):
                for first, size in ((0, full), (full, rest)):
                    cells = (pl.ds(first, size), pl.ds(half * lanes, lanes))
                    if comp == 0:
                        one = depth_ref[(2 * pair, *cells)]
                        two = depth_ref[(2 * pair + 1, *cells)]
                    else:
                        one = flow_ref[(2 * pair, comp - 1, *cells)]
                        two = flow_ref[(2 * pair + 1, comp - 1, *cells)]
                    low = lanes_low(one.shape, elements)
                    base = node_count * first + 2 * half * size
                    fields_ref[pair, comp, base : base + size, :] = jnp.where(
                        low, one, pltpu.roll(two, elements, 1)
                    )
                    fields_ref[pair, comp, base + size : base + 2 * size, :] = jnp.where(
                        low, pltpu.roll(one, elements, 1), two
                    )
        for face in range(faces):
            nodes = [int(node) for node in face_nodes[face][::-1]]
            for comp in range(3):
                stack_face(
                    fields_ref, pair, comp, nodes, members, node_count,
                    stack_ref.at[face], comp * face_rows,
                )
            turned = stack_ref[face].T
            start = pl.multiple_of((2 * pair * faces + face) * elements, 8)
            table_ref[pl.ds(start, elements), :] = turned[:elements]
            start = pl.multiple_of(((2 * pair + 1) * faces + face) * elements, 8)
            table_ref[pl.ds(start, elements), :] = turned[elements:]
        return carry

    lax.fori_loop(0, blocks // 2, one_pair, 0)
    rim_count = rim_ref.shape[1]

    def one_group(group, carry):
        for step in range(16):
            face = group * 16 + step
            edge_ref[pl.ds(face, 1), :] = table_ref[pl.ds(rim_ref[0, face], 1), :]
        return carry

    lax.fori_loop(0, rim_count // 16, one_group, 0)


def advance_kernel(
    face_nodes, node_count, members, low_start,
    own_ref, map_ref, wet_ref, breach_ref, plan_ref,
    fields_ref, table_ref, before_ref, after_ref,
    metric_ref, scale_ref, angle_ref, links_ref, high_ref, low_ref,
    depth_out, flow_out, send_ref,
    pool_ref, picked_ref, inner_ref, cos_ref, sin_ref, wall_ref, right_ref, chosen_ref, sems,
):
    blocks = depth_out.shape[0]
    elements = metric_ref.shape[2]
    lanes = 2 * elements
    rows = fields_ref.shape[2]
    full = members // 8 * 8
    rest = members - full
    face_rows = face_points * members
    block_faces = faces * elements
    local_faces = blocks * block_faces
    rim = before_ref.shape[0]
    copies = [
        pltpu.make_async_copy(table_ref, pool_ref.at[pl.ds(0, local_faces)], sems.at[0]),
        pltpu.make_async_copy(before_ref, pool_ref.at[pl.ds(local_faces, rim)], sems.at[1]),
        pltpu.make_async_copy(after_ref, pool_ref.at[pl.ds(local_faces + rim, rim)], sems.at[2]),
    ]
    for copy in copies:
        copy.start()

    angles = angle_ref[...]
    cos_ref[...] = jnp.cos(angles)
    sin_ref[...] = jnp.sin(angles)
    own_number = (
        lax.broadcasted_iota(jnp.int32, angles.shape, 0) * block_faces
        + lax.broadcasted_iota(jnp.int32, angles.shape, 1)
    )
    wall_ref[...] = jnp.where(links_ref[...] == own_number, 1.0, 0.0)
    right_ref[...] = jnp.zeros_like(right_ref)

    own = own_ref[0]

    def clear(index, carry):
        chosen_ref[index] = 0
        return carry

    lax.fori_loop(0, chosen_ref.shape[0], clear, 0)

    def choose(index, carry):
        target = plan_ref[own * blocks + index] // blocks

        @pl.when(target != own)
        def _():
            chosen_ref[target] = index

        return carry

    lax.fori_loop(0, blocks, choose, 0)
    for copy in copies:
        copy.wait()

    def one_pair(pair, carry):
        for side in range(2):
            for face in range(block_faces):
                picked_ref[side * block_faces + face : side * block_faces + face + 1, :] = pool_ref[
                    pl.ds(map_ref[2 * pair + side, face], 1), :
                ]

        def face_row(ref, face):
            first = ref[pl.ds(2 * pair, 1), :]
            second = ref[pl.ds(2 * pair + 1, 1), :]
            cells = slice(face * elements, (face + 1) * elements)
            return jnp.concatenate([first[:, cells], second[:, cells]], axis=1)

        for face in range(faces):
            nodes = [int(node) for node in face_nodes[face]]
            for comp in range(3):
                stack_face(
                    fields_ref, pair, comp, nodes, members, node_count,
                    inner_ref.at[face], comp * face_rows,
                )
            height = inner_ref[face, 0:face_rows]
            flow_x = inner_ref[face, face_rows : 2 * face_rows]
            flow_y = inner_ref[face, 2 * face_rows : 3 * face_rows]
            outside = jnp.concatenate(
                [
                    picked_ref[face * elements : (face + 1) * elements],
                    picked_ref[block_faces + face * elements : block_faces + (face + 1) * elements],
                ],
                axis=0,
            ).T
            normal_x = face_row(cos_ref, face)
            normal_y = face_row(sin_ref, face)
            wall = face_row(wall_ref, face) > 0.5
            half_scale = 0.5 * face_row(scale_ref, face)
            flow = flow_x * normal_x + flow_y * normal_y
            out_height = jnp.where(wall, height, outside[0:face_rows])
            out_x = jnp.where(
                wall, flow_x - 2.0 * flow * normal_x, outside[face_rows : 2 * face_rows]
            )
            out_y = jnp.where(
                wall, flow_y - 2.0 * flow * normal_y, outside[2 * face_rows : 3 * face_rows]
            )
            out_flow = out_x * normal_x + out_y * normal_y
            speed = flow / height
            out_speed = out_flow / out_height
            wave = jnp.maximum(
                jnp.abs(speed) + jnp.sqrt(gravity * height),
                jnp.abs(out_speed) + jnp.sqrt(gravity * out_height),
            )
            pressure = 0.5 * gravity * (height * height - out_height * out_height)
            jumps = (
                flow - out_flow + wave * (out_height - height),
                flow_x * speed - out_x * out_speed + pressure * normal_x + wave * (out_x - flow_x),
                flow_y * speed - out_y * out_speed + pressure * normal_y + wave * (out_y - flow_y),
            )
            start = 2 * rows + face * face_rows
            for comp in range(3):
                right_ref[start : start + face_rows, comp * lanes : (comp + 1) * lanes] = (
                    half_scale * jumps[comp]
                )

        factors = jnp.concatenate([metric_ref[2 * pair], metric_ref[2 * pair + 1]], axis=1)
        height = fields_ref[pair, 0]
        flow_x = fields_ref[pair, 1]
        flow_y = fields_ref[pair, 2]
        inverse = 1.0 / height
        pressure = 0.5 * gravity * height * height
        speed_x = flow_x * inverse
        speed_y = flow_y * inverse
        cross = flow_x * speed_y
        flux_f = (flow_x, flow_x * speed_x + pressure, cross)
        flux_g = (flow_y, cross, flow_y * speed_y + pressure)
        for comp in range(3):
            span = slice(comp * lanes, (comp + 1) * lanes)
            right_ref[0:rows, span] = factors[0:1] * flux_f[comp] + factors[2:3] * flux_g[comp]
            right_ref[rows : 2 * rows, span] = (
                factors[1:2] * flux_f[comp] + factors[3:4] * flux_g[comp]
            )
        right = right_ref[...]
        right_high = right.astype(jnp.bfloat16)
        right_low = (right - right_high.astype(jnp.float32)).astype(jnp.bfloat16)
        high = high_ref[...]
        tendency = (
            jnp.dot(high, right_high, preferred_element_type=jnp.float32)
            + jnp.dot(high, right_low, preferred_element_type=jnp.float32)
            + jnp.dot(
                low_ref[...], right_high[low_start:], preferred_element_type=jnp.float32
            )
        )
        row_low = lanes_low((1, lanes), elements)
        step = time_step * jnp.where(
            row_low, wet_ref[2 * pair].astype(jnp.float32), wet_ref[2 * pair + 1].astype(jnp.float32)
        )

        def inflow(member):
            return breach_rate * jnp.where(
                row_low,
                breach_ref[2 * pair, member].astype(jnp.float32),
                breach_ref[2 * pair + 1, member].astype(jnp.float32),
            )

        def inflow_rows(first, size):
            row_ids = lax.broadcasted_iota(jnp.int32, (size, lanes), 0)
            total = jnp.zeros((size, lanes), jnp.float32)
            for member in range(size):
                total = jnp.where(row_ids == member, inflow(first + member), total)
            return total

        for first, size in ((0, full), (full, rest)):
            source = inflow_rows(first, size)
            low = lanes_low((size, lanes), elements)
            for comp in range(3):
                span = slice(comp * lanes, (comp + 1) * lanes)
                for half in range(node_count // 2):
                    both = []
                    for side in range(2):
                        base = node_count * first + (2 * half + side) * size
                        change = tendency[base : base + size, span]
                        if comp == 0:
                            change = change + source
                        both.append(fields_ref[pair, comp, base : base + size, :] + step * change)
                    one = jnp.where(low, both[0], pltpu.roll(both[1], elements, 1))
                    two = jnp.where(low, pltpu.roll(both[0], elements, 1), both[1])
                    cells = (pl.ds(first, size), pl.ds(half * lanes, lanes))
                    if comp == 0:
                        depth_out[(2 * pair, *cells)] = one
                        depth_out[(2 * pair + 1, *cells)] = two
                    else:
                        flow_out[(2 * pair, comp - 1, *cells)] = one
                        flow_out[(2 * pair + 1, comp - 1, *cells)] = two
        return carry

    lax.fori_loop(0, blocks // 2, one_pair, 0)

    def one_send(device, carry):
        block = chosen_ref[device]
        for comp in range(3):
            for first, size in ((0, full), (full, rest)):
                base = 3 * first + comp * size
                if comp == 0:
                    value = depth_out[block, first : first + size, :]
                else:
                    value = flow_out[block, comp - 1, first : first + size, :]
                send_ref[device, base : base + size, :] = value
        return carry

    lax.fori_loop(0, send_ref.shape[0], one_send, 0)


def merge_kernel(source_ref, own_ref, got_ref, depth_ref, flow_ref, depth_out, flow_out):
    blocks, members, _ = depth_ref.shape
    full = members // 8 * 8
    rest = members - full

    def one_slot(slot, carry):
        source = source_ref[slot]

        @pl.when(source == own_ref[0])
        def _():
            depth_out[slot] = depth_ref[slot]
            flow_out[slot] = flow_ref[slot]

        @pl.when(source != own_ref[0])
        def _():
            for comp in range(3):
                for first, size in ((0, full), (full, rest)):
                    base = 3 * first + comp * size
                    value = got_ref[source, base : base + size, :]
                    if comp == 0:
                        depth_out[slot, first : first + size, :] = value
                    else:
                        flow_out[slot, comp - 1, first : first + size, :] = value

        return carry

    lax.fori_loop(0, blocks, one_slot, 0)


def body(
    water_depth,
    momentum,
    metric,
    face_scale,
    face_angle,
    face_map,
    rim_faces,
    wet_blocks,
    breach,
    block_plan,
):
    face_nodes = node_tables()[3]
    node_count = int(face_nodes.max()) + 1
    blocks, members, node_cells = water_depth.shape
    elements = node_cells // node_count
    lanes = 2 * elements
    rows = round_up(node_count * members, 16)
    block_faces = faces * elements
    local_faces = blocks * block_faces
    rim_count = rim_faces.shape[1]
    rim = rim_count // 2
    own_index = lax.axis_index("mesh")
    devices = lax.axis_size("mesh")
    params = pltpu.CompilerParams(vmem_limit_bytes=48 * 2**20)
    f32 = jnp.float32

    fields, table, edge = pl.pallas_call(
        lambda *refs: layout_kernel(face_nodes, node_count, *refs),
        out_shape=(
            jax.ShapeDtypeStruct((blocks // 2, 3, rows, lanes), f32),
            jax.ShapeDtypeStruct((local_faces, lanes), f32),
            jax.ShapeDtypeStruct((rim_count, lanes), f32),
        ),
        in_specs=[VMEM, VMEM, SMEM],
        out_specs=(VMEM, VMEM, VMEM),
        scratch_shapes=[pltpu.VMEM((faces, lanes, lanes), f32)],
        compiler_params=params,
    )(water_depth, momentum, rim_faces)

    ends = devices - 1
    from_before = lax.ppermute(edge[rim:], "mesh", [(i, i + 1) for i in range(ends)])
    from_after = lax.ppermute(edge[:rim], "mesh", [(i + 1, i) for i in range(ends)])

    high, low = combined_matrix(members, rows, node_count)
    low_start = 2 * rows if not np.any(low[:, : 2 * rows].astype(np.float32)) else 0
    own = jnp.reshape(own_index.astype(jnp.int32), (1,))
    send_rows = round_up(3 * members, 8)
    depth, flow, send = pl.pallas_call(
        lambda *refs: advance_kernel(face_nodes, node_count, members, low_start, *refs),
        out_shape=(
            jax.ShapeDtypeStruct(water_depth.shape, f32),
            jax.ShapeDtypeStruct(momentum.shape, f32),
            jax.ShapeDtypeStruct((devices, send_rows, node_cells), f32),
        ),
        in_specs=[SMEM] * 5 + [VMEM, ANY, ANY, ANY] + [VMEM] * 6,
        out_specs=(VMEM, VMEM, VMEM),
        scratch_shapes=[
            pltpu.VMEM((local_faces + rim_count, lanes), f32),
            pltpu.VMEM((2 * block_faces, lanes), f32),
            pltpu.VMEM((faces, lanes, lanes), f32),
            pltpu.VMEM((blocks, block_faces), f32),
            pltpu.VMEM((blocks, block_faces), f32),
            pltpu.VMEM((blocks, block_faces), f32),
            pltpu.VMEM((high.shape[1], 3 * lanes), f32),
            pltpu.SMEM((devices,), jnp.int32),
            pltpu.SemaphoreType.DMA((3,)),
        ],
        compiler_params=params,
    )(
        own, face_map, wet_blocks, breach, block_plan,
        fields, table, from_before, from_after,
        metric, face_scale, face_angle, face_map, jnp.asarray(high), jnp.asarray(low[:, low_start:]),
    )

    got = lax.all_to_all(send, "mesh", split_axis=0, concat_axis=0, tiled=True)
    slot_ids = own_index * blocks + jnp.arange(blocks, dtype=jnp.int32)
    every_slot = jnp.arange(block_plan.shape[0], dtype=jnp.int32)
    source = jnp.sum(
        jnp.where(block_plan[None, :] == slot_ids[:, None], every_slot[None, :], 0), axis=1
    ) // blocks
    return pl.pallas_call(
        merge_kernel,
        out_shape=(
            jax.ShapeDtypeStruct(water_depth.shape, f32),
            jax.ShapeDtypeStruct(momentum.shape, f32),
        ),
        in_specs=[SMEM, SMEM, VMEM, VMEM, VMEM],
        out_specs=(VMEM, VMEM),
        compiler_params=params,
    )(source, own, got, depth, flow)


def solution(mesh):
    in_specs = (
        P(("groups", "mesh"), None, None),
        P(("groups", "mesh"), None, None, None),
        P(("groups", "mesh"), None, None),
        P(("groups", "mesh"), None),
        P(("groups", "mesh"), None),
        P(("groups", "mesh"), None),
        P(("groups", "mesh"), None),
        P(("groups", "mesh")),
        P(("groups", "mesh"), None),
        P("groups"),
    )
    out_specs = (P(("groups", "mesh"), None, None), P(("groups", "mesh"), None, None, None))
    return jax.shard_map(body, mesh=mesh, in_specs=in_specs, out_specs=out_specs, check_vma=False)
```

```python
import math

import jax
import jax.numpy as jnp
import numpy as np
import ml_dtypes
from jax import lax
from jax.experimental import pallas as pl
from jax.experimental.pallas import tpu as pltpu
from jax.sharding import PartitionSpec as P

time_step = 0.01
gravity = 1.0
breach_rate = 5.0


SMEM = pl.BlockSpec(memory_space=pltpu.SMEM)
VMEM = pl.BlockSpec(memory_space=pltpu.VMEM)
ANY = pl.BlockSpec(memory_space=pl.ANY)
faces, face_points = 3, 4


def gauss_solve(matrix, right):
    dimension = matrix.shape[0]
    augmented = np.concatenate([np.array(matrix) * 1.0, np.array(right) * 1.0], axis=1)
    for pivot_col in range(dimension):
        largest = pivot_col + int(np.argmax(np.abs(augmented[pivot_col:, pivot_col])))
        swapped = augmented[[largest, pivot_col]]
        augmented[[pivot_col, largest]] = swapped
        augmented[pivot_col] = augmented[pivot_col] / augmented[pivot_col, pivot_col]
        for row_id in range(dimension):
            if row_id != pivot_col:
                augmented[row_id] = (
                    augmented[row_id] - augmented[row_id, pivot_col] * augmented[pivot_col]
                )
    return augmented[:, dimension:]


def node_tables():
    points = np.array(
        [(across / 3.0, upward / 3.0) for upward in range(4) for across in range(4 - upward)]
    )
    powers = [(power_r, power_s) for power_r in range(4) for power_s in range(4 - power_r)]
    vander = np.zeros((10, 10))
    grad_r = np.zeros((10, 10))
    grad_s = np.zeros((10, 10))
    mono_mass = np.zeros((10, 10))
    for column, (power_r, power_s) in enumerate(powers):
        vander[:, column] = points[:, 0] ** power_r * points[:, 1] ** power_s
        if power_r > 0:
            grad_r[:, column] = power_r * points[:, 0] ** (power_r - 1) * points[:, 1] ** power_s
        if power_s > 0:
            grad_s[:, column] = power_s * points[:, 0] ** power_r * points[:, 1] ** (power_s - 1)
        for second_column, (other_r, other_s) in enumerate(powers):
            mono_mass[column, second_column] = (
                math.factorial(power_r + other_r)
                * math.factorial(power_s + other_s)
                / math.factorial(power_r + other_r + power_s + other_s + 2)
            )
    inverse = gauss_solve(vander, np.eye(10))
    mass_matrix = inverse.T @ mono_mass @ inverse
    line_points = np.arange(4) / 3.0
    line_vander = line_points[:, None] ** np.arange(4)[None, :]
    hilbert = 1.0 / (np.arange(4)[:, None] + np.arange(4)[None, :] + 1.0)
    line_inverse = gauss_solve(line_vander, np.eye(4))
    edge_mass = line_inverse.T @ hilbert @ line_inverse
    face_nodes = np.array([[0, 1, 2, 3], [3, 6, 8, 9], [9, 7, 4, 0]])
    edge_embed = np.zeros((10, 12))
    for face_id in range(3):
        for node_id in range(4):
            edge_embed[face_nodes[face_id, node_id], 4 * face_id : 4 * face_id + 4] += edge_mass[
                node_id
            ]
    lifting = gauss_solve(mass_matrix, edge_embed).reshape(10, 3, 4)
    return (
        np.asarray(grad_r @ inverse, np.float32),
        np.asarray(grad_s @ inverse, np.float32),
        np.asarray(lifting, np.float32),
        face_nodes,
    )


def round_up(count, step):
    return -(-count // step) * step


def combined_matrix(members, rows, node_count):
    deriv_r, deriv_s, lifting, _ = node_tables()
    full = members // 8 * 8
    rest = members - full
    face_rows = face_points * members
    columns = 2 * rows + round_up(faces * face_rows, 16)

    def place(point, member, points):
        if member < full:
            return point * full + member
        return points * full + point * rest + member - full

    table = np.zeros((rows, columns), np.float32)
    for member in range(members):
        for node in range(node_count):
            row = place(node, member, node_count)
            for other in range(node_count):
                column = place(other, member, node_count)
                table[row, column] = -deriv_r[node, other]
                table[row, rows + column] = -deriv_s[node, other]
            for face in range(faces):
                for point in range(face_points):
                    column = 2 * rows + face * face_rows + place(point, member, face_points)
                    table[row, column] = lifting[node, face, point]
    high = table.astype(ml_dtypes.bfloat16)
    low = (table - high.astype(np.float32)).astype(ml_dtypes.bfloat16)
    return high, low


def lanes_low(shape, elements):
    return lax.broadcasted_iota(jnp.int32, shape, len(shape) - 1) < elements


def stack_face(fields_ref, pair, comp, nodes, members, node_count, out_ref, start):
    full = members // 8 * 8
    rest = members - full
    for point, node in enumerate(nodes):
        out_ref[start + point * full : start + (point + 1) * full, :] = fields_ref[
            pair, comp, node * full : (node + 1) * full, :
        ]
    base = node_count * full
    tail = start + len(nodes) * full
    for point, node in enumerate(nodes):
        out_ref[tail + point * rest : tail + (point + 1) * rest, :] = fields_ref[
            pair, comp, base + node * rest : base + (node + 1) * rest, :
        ]


def lay_out(
    face_nodes, node_count, order_ref, depth_ref, flow_ref, rim_ref,
    fields_ref, table_ref, edge_ref, stack_ref,
):
    blocks, members, node_cells = depth_ref.shape
    elements = node_cells // node_count
    lanes = 2 * elements
    full = members // 8 * 8
    rest = members - full
    used = node_count * members
    rows = fields_ref.shape[2]
    face_rows = face_points * members
    stack_ref[...] = jnp.zeros_like(stack_ref)

    def one_pair(pair, carry):
        sides = (order_ref[2 * pair], order_ref[2 * pair + 1])
        for comp in range(3):
            fields_ref[pair, comp, used:rows, :] = jnp.ones((rows - used, lanes), jnp.float32)
            for half in range(node_count // 2):
                for first, size in ((0, full), (full, rest)):
                    cells = (pl.ds(first, size), pl.ds(half * lanes, lanes))
                    if comp == 0:
                        one = depth_ref[(sides[0], *cells)]
                        two = depth_ref[(sides[1], *cells)]
                    else:
                        one = flow_ref[(sides[0], comp - 1, *cells)]
                        two = flow_ref[(sides[1], comp - 1, *cells)]
                    low = lanes_low(one.shape, elements)
                    base = node_count * first + 2 * half * size
                    fields_ref[pair, comp, base : base + size, :] = jnp.where(
                        low, one, pltpu.roll(two, elements, 1)
                    )
                    fields_ref[pair, comp, base + size : base + 2 * size, :] = jnp.where(
                        low, pltpu.roll(one, elements, 1), two
                    )
        for face in range(faces):
            nodes = [int(node) for node in face_nodes[face][::-1]]
            for comp in range(3):
                stack_face(
                    fields_ref, pair, comp, nodes, members, node_count,
                    stack_ref.at[face], comp * face_rows,
                )
            turned = stack_ref[face].T
            start = pl.multiple_of((2 * pair * faces + face) * elements, 8)
            table_ref[pl.ds(start, elements), :] = turned[:elements]
            start = pl.multiple_of(((2 * pair + 1) * faces + face) * elements, 8)
            table_ref[pl.ds(start, elements), :] = turned[elements:]
        return carry

    lax.fori_loop(0, blocks // 2, one_pair, 0)
    rim_count = rim_ref.shape[0]

    def one_group(group, carry):
        for step in range(16):
            face = group * 16 + step
            edge_ref[pl.ds(face, 1), :] = table_ref[pl.ds(rim_ref[face], 1), :]
        return carry

    lax.fori_loop(0, rim_count // 16, one_group, 0)


def section_kernel(
    face_nodes, node_count, members, low_start, early,
    order_ref, map_ref, rim_ref, wet_ref, breach_ref, chosen_ref, slot_ref, source_ref,
    depth_ref, flow_ref, metric_ref, scale_ref, angle_ref, links_ref, high_ref, low_ref,
    depth_out, flow_out,
    fields_ref, pool_ref, edge_ref, before_ref, after_ref, picked_ref, inner_ref,
    cos_ref, sin_ref, wall_ref, right_ref, moved_ref, send_ref, got_ref,
    rim_sems, send_sems, got_sems,
):
    blocks = depth_out.shape[0]
    elements = metric_ref.shape[2]
    lanes = 2 * elements
    rows = fields_ref.shape[2]
    full = members // 8 * 8
    rest = members - full
    face_rows = face_points * members
    block_faces = faces * elements
    local_faces = blocks * block_faces
    rim = before_ref.shape[0]
    devices = got_ref.shape[0]
    own = lax.axis_index("mesh")
    mesh_type = pl.DeviceIdType.MESH

    barrier = pltpu.get_barrier_semaphore()
    for step in range(1, devices):
        pl.semaphore_signal(
            barrier, inc=1, device_id={"mesh": lax.rem(own + step, devices)},
            device_id_type=mesh_type,
        )

    lay_out(
        face_nodes, node_count, order_ref, depth_ref, flow_ref, rim_ref,
        fields_ref, pool_ref, edge_ref, inner_ref,
    )
    pl.semaphore_wait(barrier, devices - 1)

    to_next = pltpu.make_async_remote_copy(
        src_ref=edge_ref.at[pl.ds(rim, rim)], dst_ref=before_ref,
        send_sem=rim_sems.at[0], recv_sem=rim_sems.at[1],
        device_id={"mesh": lax.rem(own + 1, devices)}, device_id_type=mesh_type,
    )
    to_before = pltpu.make_async_remote_copy(
        src_ref=edge_ref.at[pl.ds(0, rim)], dst_ref=after_ref,
        send_sem=rim_sems.at[2], recv_sem=rim_sems.at[3],
        device_id={"mesh": lax.rem(own + devices - 1, devices)}, device_id_type=mesh_type,
    )

    @pl.when(own < devices - 1)
    def _():
        to_next.start()

    @pl.when(own > 0)
    def _():
        to_before.start()

    angles = angle_ref[...]
    cos_ref[...] = jnp.cos(angles)
    sin_ref[...] = jnp.sin(angles)
    own_number = (
        lax.broadcasted_iota(jnp.int32, angles.shape, 0) * block_faces
        + lax.broadcasted_iota(jnp.int32, angles.shape, 1)
    )
    wall_ref[...] = jnp.where(links_ref[...] == own_number, 1.0, 0.0)
    right_ref[...] = jnp.zeros_like(right_ref)
    moved_ref[...] = jnp.zeros_like(moved_ref)
    got_ref[own] = jnp.zeros(got_ref.shape[1:], jnp.float32)

    @pl.when(own > 0)
    def _():
        to_next.wait_recv()
        pool_ref[local_faces : local_faces + rim, :] = before_ref[...]

    @pl.when(own < devices - 1)
    def _():
        to_before.wait_recv()
        pool_ref[local_faces + rim : local_faces + 2 * rim, :] = after_ref[...]

    def one_pair(pair, carry):
        sides = (order_ref[2 * pair], order_ref[2 * pair + 1])
        for side in range(2):
            for face in range(block_faces):
                picked_ref[side * block_faces + face : side * block_faces + face + 1, :] = pool_ref[
                    pl.ds(map_ref[sides[side], face], 1), :
                ]

        def face_row(ref, face):
            first = ref[pl.ds(sides[0], 1), :]
            second = ref[pl.ds(sides[1], 1), :]
            cells = slice(face * elements, (face + 1) * elements)
            return jnp.concatenate([first[:, cells], second[:, cells]], axis=1)

        for face in range(faces):
            nodes = [int(node) for node in face_nodes[face]]
            for comp in range(3):
                stack_face(
                    fields_ref, pair, comp, nodes, members, node_count,
                    inner_ref.at[face], comp * face_rows,
                )
            height = inner_ref[face, 0:face_rows]
            flow_x = inner_ref[face, face_rows : 2 * face_rows]
            flow_y = inner_ref[face, 2 * face_rows : 3 * face_rows]
            outside = jnp.concatenate(
                [
                    picked_ref[face * elements : (face + 1) * elements],
                    picked_ref[block_faces + face * elements : block_faces + (face + 1) * elements],
                ],
                axis=0,
            ).T
            normal_x = face_row(cos_ref, face)
            normal_y = face_row(sin_ref, face)
            wall = face_row(wall_ref, face) > 0.5
            half_scale = 0.5 * face_row(scale_ref, face)
            flow = flow_x * normal_x + flow_y * normal_y
            out_height = jnp.where(wall, height, outside[0:face_rows])
            out_x = jnp.where(
                wall, flow_x - 2.0 * flow * normal_x, outside[face_rows : 2 * face_rows]
            )
            out_y = jnp.where(
                wall, flow_y - 2.0 * flow * normal_y, outside[2 * face_rows : 3 * face_rows]
            )
            out_flow = out_x * normal_x + out_y * normal_y
            speed = flow / height
            out_speed = out_flow / out_height
            wave = jnp.maximum(
                jnp.abs(speed) + jnp.sqrt(gravity * height),
                jnp.abs(out_speed) + jnp.sqrt(gravity * out_height),
            )
            pressure = 0.5 * gravity * (height * height - out_height * out_height)
            jumps = (
                flow - out_flow + wave * (out_height - height),
                flow_x * speed - out_x * out_speed + pressure * normal_x + wave * (out_x - flow_x),
                flow_y * speed - out_y * out_speed + pressure * normal_y + wave * (out_y - flow_y),
            )
            start = 2 * rows + face * face_rows
            for comp in range(3):
                right_ref[start : start + face_rows, comp * lanes : (comp + 1) * lanes] = (
                    half_scale * jumps[comp]
                )

        factors = jnp.concatenate([metric_ref[sides[0]], metric_ref[sides[1]]], axis=1)
        height = fields_ref[pair, 0]
        flow_x = fields_ref[pair, 1]
        flow_y = fields_ref[pair, 2]
        inverse = 1.0 / height
        pressure = 0.5 * gravity * height * height
        speed_x = flow_x * inverse
        speed_y = flow_y * inverse
        cross = flow_x * speed_y
        flux_f = (flow_x, flow_x * speed_x + pressure, cross)
        flux_g = (flow_y, cross, flow_y * speed_y + pressure)
        for comp in range(3):
            span = slice(comp * lanes, (comp + 1) * lanes)
            right_ref[0:rows, span] = factors[0:1] * flux_f[comp] + factors[2:3] * flux_g[comp]
            right_ref[rows : 2 * rows, span] = (
                factors[1:2] * flux_f[comp] + factors[3:4] * flux_g[comp]
            )
        right = right_ref[...]
        right_high = right.astype(jnp.bfloat16)
        right_low = (right - right_high.astype(jnp.float32)).astype(jnp.bfloat16)
        high = high_ref[...]
        tendency = (
            jnp.dot(high, right_high, preferred_element_type=jnp.float32)
            + jnp.dot(high, right_low, preferred_element_type=jnp.float32)
            + jnp.dot(
                low_ref[...], right_high[low_start:], preferred_element_type=jnp.float32
            )
        )
        row_low = lanes_low((1, lanes), elements)
        step = time_step * jnp.where(
            row_low, wet_ref[sides[0]].astype(jnp.float32), wet_ref[sides[1]].astype(jnp.float32)
        )

        def inflow(member):
            return breach_rate * jnp.where(
                row_low,
                breach_ref[sides[0], member].astype(jnp.float32),
                breach_ref[sides[1], member].astype(jnp.float32),
            )

        def inflow_rows(first, size):
            row_ids = lax.broadcasted_iota(jnp.int32, (size, lanes), 0)
            total = jnp.zeros((size, lanes), jnp.float32)
            for member in range(size):
                total = jnp.where(row_ids == member, inflow(first + member), total)
            return total

        for first, size in ((0, full), (full, rest)):
            source = inflow_rows(first, size)
            low = lanes_low((size, lanes), elements)
            for comp in range(3):
                span = slice(comp * lanes, (comp + 1) * lanes)
                for half in range(node_count // 2):
                    both = []
                    for side in range(2):
                        base = node_count * first + (2 * half + side) * size
                        change = tendency[base : base + size, span]
                        if comp == 0:
                            change = change + source
                        both.append(fields_ref[pair, comp, base : base + size, :] + step * change)
                    one = jnp.where(low, both[0], pltpu.roll(both[1], elements, 1))
                    two = jnp.where(low, pltpu.roll(both[0], elements, 1), both[1])
                    base = 3 * first + comp * size
                    span_out = slice(half * lanes, (half + 1) * lanes)
                    moved_ref[2 * pair, base : base + size, span_out] = one
                    moved_ref[2 * pair + 1, base : base + size, span_out] = two
        return carry


    lax.fori_loop(0, early, one_pair, 0)

    def one_send(device, carry):
        send_ref[device] = moved_ref[chosen_ref[device]]
        return carry

    lax.fori_loop(0, devices, one_send, 0)
    sends = []
    for step in sorted(range(1, devices), key=lambda step: abs(step - devices // 2)):
        target = lax.rem(own + step, devices)
        sends.append(
            pltpu.make_async_remote_copy(
                src_ref=send_ref.at[target], dst_ref=got_ref.at[own],
                send_sem=send_sems.at[target], recv_sem=got_sems.at[own],
                device_id={"mesh": target}, device_id_type=mesh_type,
            )
        )
    for copy in sends:
        copy.start()

    lax.fori_loop(early, blocks // 2, one_pair, 0)

    for step in range(1, devices):
        origin = lax.rem(own + step, devices)
        pltpu.make_async_remote_copy(
            src_ref=send_ref.at[origin], dst_ref=got_ref.at[origin],
            send_sem=send_sems.at[origin], recv_sem=got_sems.at[origin],
            device_id={"mesh": origin}, device_id_type=mesh_type,
        ).wait_recv()

    def one_slot(slot, carry):
        stays = source_ref[slot] == own
        for comp in range(3):
            for first, size in ((0, full), (full, rest)):
                base = 3 * first + comp * size
                span = slice(base, base + size)
                value = jnp.where(
                    stays, moved_ref[slot_ref[slot], span, :], got_ref[source_ref[slot], span, :]
                )
                if comp == 0:
                    depth_out[slot, first : first + size, :] = value
                else:
                    flow_out[slot, comp - 1, first : first + size, :] = value
        return carry

    lax.fori_loop(0, blocks, one_slot, 0)
    for copy in sends:
        copy.wait_send()

    @pl.when(own < devices - 1)
    def _():
        to_next.wait_send()

    @pl.when(own > 0)
    def _():
        to_before.wait_send()


def body(
    water_depth,
    momentum,
    metric,
    face_scale,
    face_angle,
    face_map,
    rim_faces,
    wet_blocks,
    breach,
    block_plan,
):
    face_nodes = node_tables()[3]
    node_count = int(face_nodes.max()) + 1
    blocks, members, node_cells = water_depth.shape
    elements = node_cells // node_count
    lanes = 2 * elements
    rows = round_up(node_count * members, 16)
    block_faces = faces * elements
    local_faces = blocks * block_faces
    rim_count = rim_faces.shape[1]
    rim = rim_count // 2
    own = lax.axis_index("mesh").astype(jnp.int32)
    devices = lax.axis_size("mesh")
    f32 = jnp.float32

    local_ids = jnp.arange(blocks, dtype=jnp.int32)
    targets = lax.dynamic_slice_in_dim(block_plan, own * blocks, blocks) // blocks
    stays = (targets == own).astype(jnp.int32)
    keys = stays * blocks + local_ids
    place = jnp.sum((keys[None, :] < keys[:, None]).astype(jnp.int32), axis=1)
    order = jnp.sum(jnp.where(place[None, :] == local_ids[:, None], local_ids[None, :], 0), axis=1)
    device_ids = jnp.arange(devices, dtype=jnp.int32)
    chosen = jnp.sum(jnp.where(targets[None, :] == device_ids[:, None], place[None, :], 0), axis=1)
    chosen = jnp.where(device_ids == own, 0, chosen)
    slot_ids = own * blocks + local_ids
    every_slot = jnp.arange(block_plan.shape[0], dtype=jnp.int32)
    source = jnp.sum(
        jnp.where(block_plan[None, :] == slot_ids[:, None], every_slot[None, :], 0), axis=1
    )
    origin = jnp.clip(source - own * blocks, 0, blocks - 1)
    slot_place = jnp.sum(jnp.where(origin[:, None] == local_ids[None, :], place[None, :], 0), axis=1)
    source = source // blocks

    def to_place(numbers):
        block = numbers // block_faces
        shift = jnp.zeros_like(numbers)
        for index in range(blocks):
            shift = jnp.where(block == index, (place[index] - index) * block_faces, shift)
        return numbers + shift

    high, low = combined_matrix(members, rows, node_count)
    low_start = 2 * rows if not np.any(low[:, : 2 * rows].astype(np.float32)) else 0
    early = min(-(-(devices // 2) // 2), blocks // 2)
    send_rows = round_up(3 * members, 8)
    return pl.pallas_call(
        lambda *refs: section_kernel(face_nodes, node_count, members, low_start, early, *refs),
        out_shape=(
            jax.ShapeDtypeStruct(water_depth.shape, f32),
            jax.ShapeDtypeStruct(momentum.shape, f32),
        ),
        in_specs=[SMEM] * 8 + [VMEM] * 8,
        out_specs=(VMEM, VMEM),
        scratch_shapes=[
            pltpu.VMEM((blocks // 2, 3, rows, lanes), f32),
            pltpu.VMEM((local_faces + rim_count, lanes), f32),
            pltpu.VMEM((rim_count, lanes), f32),
            pltpu.VMEM((rim, lanes), f32),
            pltpu.VMEM((rim, lanes), f32),
            pltpu.VMEM((2 * block_faces, lanes), f32),
            pltpu.VMEM((faces, lanes, lanes), f32),
            pltpu.VMEM((blocks, block_faces), f32),
            pltpu.VMEM((blocks, block_faces), f32),
            pltpu.VMEM((blocks, block_faces), f32),
            pltpu.VMEM((high.shape[1], 3 * lanes), f32),
            pltpu.VMEM((blocks, send_rows, node_cells), f32),
            pltpu.VMEM((devices, send_rows, node_cells), f32),
            pltpu.VMEM((devices, send_rows, node_cells), f32),
            pltpu.SemaphoreType.DMA((4,)),
            pltpu.SemaphoreType.DMA((devices,)),
            pltpu.SemaphoreType.DMA((devices,)),
        ],
        compiler_params=pltpu.CompilerParams(
            vmem_limit_bytes=48 * 2**20, collective_id=0, has_side_effects=True
        ),
    )(
        order, to_place(face_map), to_place(rim_faces.reshape(-1)), wet_blocks, breach, chosen,
        slot_place, source, water_depth, momentum, metric, face_scale, face_angle, face_map,
        jnp.asarray(high), jnp.asarray(low[:, low_start:]),
    )


def solution(mesh):
    in_specs = (
        P(("groups", "mesh"), None, None),
        P(("groups", "mesh"), None, None, None),
        P(("groups", "mesh"), None, None),
        P(("groups", "mesh"), None),
        P(("groups", "mesh"), None),
        P(("groups", "mesh"), None),
        P(("groups", "mesh"), None),
        P(("groups", "mesh")),
        P(("groups", "mesh"), None),
        P("groups"),
    )
    out_specs = (P(("groups", "mesh"), None, None), P(("groups", "mesh"), None, None, None))
    return jax.shard_map(body, mesh=mesh, in_specs=in_specs, out_specs=out_specs, check_vma=False)
```

```python
import math

import jax
import jax.numpy as jnp
import numpy as np
import ml_dtypes
from jax import lax
from jax.experimental import pallas as pl
from jax.experimental.pallas import tpu as pltpu
from jax.sharding import PartitionSpec as P

time_step = 0.01
gravity = 1.0
breach_rate = 5.0


SMEM = pl.BlockSpec(memory_space=pltpu.SMEM)
VMEM = pl.BlockSpec(memory_space=pltpu.VMEM)
ANY = pl.BlockSpec(memory_space=pl.ANY)
faces, face_points = 3, 4


def gauss_solve(matrix, right):
    dimension = matrix.shape[0]
    augmented = np.concatenate([np.array(matrix) * 1.0, np.array(right) * 1.0], axis=1)
    for pivot_col in range(dimension):
        largest = pivot_col + int(np.argmax(np.abs(augmented[pivot_col:, pivot_col])))
        swapped = augmented[[largest, pivot_col]]
        augmented[[pivot_col, largest]] = swapped
        augmented[pivot_col] = augmented[pivot_col] / augmented[pivot_col, pivot_col]
        for row_id in range(dimension):
            if row_id != pivot_col:
                augmented[row_id] = (
                    augmented[row_id] - augmented[row_id, pivot_col] * augmented[pivot_col]
                )
    return augmented[:, dimension:]


def node_tables():
    points = np.array(
        [(across / 3.0, upward / 3.0) for upward in range(4) for across in range(4 - upward)]
    )
    powers = [(power_r, power_s) for power_r in range(4) for power_s in range(4 - power_r)]
    vander = np.zeros((10, 10))
    grad_r = np.zeros((10, 10))
    grad_s = np.zeros((10, 10))
    mono_mass = np.zeros((10, 10))
    for column, (power_r, power_s) in enumerate(powers):
        vander[:, column] = points[:, 0] ** power_r * points[:, 1] ** power_s
        if power_r > 0:
            grad_r[:, column] = power_r * points[:, 0] ** (power_r - 1) * points[:, 1] ** power_s
        if power_s > 0:
            grad_s[:, column] = power_s * points[:, 0] ** power_r * points[:, 1] ** (power_s - 1)
        for second_column, (other_r, other_s) in enumerate(powers):
            mono_mass[column, second_column] = (
                math.factorial(power_r + other_r)
                * math.factorial(power_s + other_s)
                / math.factorial(power_r + other_r + power_s + other_s + 2)
            )
    inverse = gauss_solve(vander, np.eye(10))
    mass_matrix = inverse.T @ mono_mass @ inverse
    line_points = np.arange(4) / 3.0
    line_vander = line_points[:, None] ** np.arange(4)[None, :]
    hilbert = 1.0 / (np.arange(4)[:, None] + np.arange(4)[None, :] + 1.0)
    line_inverse = gauss_solve(line_vander, np.eye(4))
    edge_mass = line_inverse.T @ hilbert @ line_inverse
    face_nodes = np.array([[0, 1, 2, 3], [3, 6, 8, 9], [9, 7, 4, 0]])
    edge_embed = np.zeros((10, 12))
    for face_id in range(3):
        for node_id in range(4):
            edge_embed[face_nodes[face_id, node_id], 4 * face_id : 4 * face_id + 4] += edge_mass[
                node_id
            ]
    lifting = gauss_solve(mass_matrix, edge_embed).reshape(10, 3, 4)
    return (
        np.asarray(grad_r @ inverse, np.float32),
        np.asarray(grad_s @ inverse, np.float32),
        np.asarray(lifting, np.float32),
        face_nodes,
    )


def round_up(count, step):
    return -(-count // step) * step


def combined_matrix(members, rows, node_count):
    deriv_r, deriv_s, lifting, _ = node_tables()
    full = members // 8 * 8
    rest = members - full
    face_rows = face_points * members
    columns = 2 * rows + round_up(faces * face_rows, 16)

    def place(point, member, points):
        if member < full:
            return point * full + member
        return points * full + point * rest + member - full

    table = np.zeros((rows, columns), np.float32)
    for member in range(members):
        for node in range(node_count):
            row = place(node, member, node_count)
            for other in range(node_count):
                column = place(other, member, node_count)
                table[row, column] = -deriv_r[node, other]
                table[row, rows + column] = -deriv_s[node, other]
            for face in range(faces):
                for point in range(face_points):
                    column = 2 * rows + face * face_rows + place(point, member, face_points)
                    table[row, column] = lifting[node, face, point]
    high = table.astype(ml_dtypes.bfloat16)
    low = (table - high.astype(np.float32)).astype(ml_dtypes.bfloat16)
    return high, low


def lanes_low(shape, elements):
    return lax.broadcasted_iota(jnp.int32, shape, len(shape) - 1) < elements


def stack_face(fields_ref, pair, comp, nodes, members, node_count, out_ref, start):
    full = members // 8 * 8
    rest = members - full
    for point, node in enumerate(nodes):
        out_ref[start + point * full : start + (point + 1) * full, :] = fields_ref[
            pair, comp, node * full : (node + 1) * full, :
        ]
    base = node_count * full
    tail = start + len(nodes) * full
    for point, node in enumerate(nodes):
        out_ref[tail + point * rest : tail + (point + 1) * rest, :] = fields_ref[
            pair, comp, base + node * rest : base + (node + 1) * rest, :
        ]


def lay_out(
    face_nodes, node_count, order_ref, place_ref, depth_ref, flow_ref, rim_ref,
    fields_ref, table_ref, edge_ref, stack_ref,
):
    blocks, members, node_cells = depth_ref.shape
    elements = node_cells // node_count
    lanes = 2 * elements
    full = members // 8 * 8
    rest = members - full
    used = node_count * members
    rows = fields_ref.shape[2]
    face_rows = face_points * members
    stack_ref[...] = jnp.zeros_like(stack_ref)

    def one_pair(pair, carry):
        sides = (order_ref[2 * pair], order_ref[2 * pair + 1])
        for comp in range(3):
            fields_ref[pair, comp, used:rows, :] = jnp.ones((rows - used, lanes), jnp.float32)
            for half in range(node_count // 2):
                for first, size in ((0, full), (full, rest)):
                    cells = (pl.ds(first, size), pl.ds(half * lanes, lanes))
                    if comp == 0:
                        one = depth_ref[(sides[0], *cells)]
                        two = depth_ref[(sides[1], *cells)]
                    else:
                        one = flow_ref[(sides[0], comp - 1, *cells)]
                        two = flow_ref[(sides[1], comp - 1, *cells)]
                    low = lanes_low(one.shape, elements)
                    base = node_count * first + 2 * half * size
                    fields_ref[pair, comp, base : base + size, :] = jnp.where(
                        low, one, pltpu.roll(two, elements, 1)
                    )
                    fields_ref[pair, comp, base + size : base + 2 * size, :] = jnp.where(
                        low, pltpu.roll(one, elements, 1), two
                    )
        for face in range(faces):
            nodes = [int(node) for node in face_nodes[face][::-1]]
            for comp in range(3):
                stack_face(
                    fields_ref, pair, comp, nodes, members, node_count,
                    stack_ref.at[face], comp * face_rows,
                )
            turned = stack_ref[face].T
            start = pl.multiple_of((2 * pair * faces + face) * elements, 8)
            table_ref[pl.ds(start, elements), :] = turned[:elements]
            start = pl.multiple_of(((2 * pair + 1) * faces + face) * elements, 8)
            table_ref[pl.ds(start, elements), :] = turned[elements:]
        return carry

    lax.fori_loop(0, blocks // 2, one_pair, 0)
    rim_count = rim_ref.shape[1]
    block_faces = faces * elements

    def one_group(group, carry):
        for step in range(16):
            face = group * 16 + step
            number = rim_ref[0, face]
            block = number // block_faces
            number = number + (place_ref[block] - block) * block_faces
            edge_ref[pl.ds(face, 1), :] = table_ref[pl.ds(number, 1), :]
        return carry

    lax.fori_loop(0, rim_count // 16, one_group, 0)


def section_kernel(
    face_nodes, node_count, members, low_start, early,
    order_ref, place_ref, map_ref, rim_ref, wet_ref, breach_ref, chosen_ref, slot_ref, source_ref,
    depth_ref, flow_ref, metric_ref, scale_ref, angle_ref, links_ref, high_ref, low_ref,
    depth_out, flow_out,
    fields_ref, pool_ref, edge_ref, before_ref, after_ref, picked_ref, inner_ref,
    cos_ref, sin_ref, wall_ref, right_ref, moved_ref, send_ref, got_ref,
    rim_sems, send_sems, got_sems,
):
    blocks = depth_out.shape[0]
    elements = metric_ref.shape[2]
    lanes = 2 * elements
    rows = fields_ref.shape[2]
    full = members // 8 * 8
    rest = members - full
    face_rows = face_points * members
    halves = node_count // 2
    block_faces = faces * elements
    local_faces = blocks * block_faces
    rim = before_ref.shape[0]
    devices = got_ref.shape[0]
    own = lax.axis_index("mesh")
    mesh_type = pl.DeviceIdType.MESH

    barrier = pltpu.get_barrier_semaphore()
    for step in range(1, devices):
        pl.semaphore_signal(
            barrier, inc=1, device_id={"mesh": lax.rem(own + step, devices)},
            device_id_type=mesh_type,
        )

    lay_out(
        face_nodes, node_count, order_ref, place_ref, depth_ref, flow_ref, rim_ref,
        fields_ref, pool_ref, edge_ref, inner_ref,
    )
    pl.semaphore_wait(barrier, devices - 1)

    to_next = pltpu.make_async_remote_copy(
        src_ref=edge_ref.at[pl.ds(rim, rim)], dst_ref=before_ref,
        send_sem=rim_sems.at[0], recv_sem=rim_sems.at[1],
        device_id={"mesh": lax.rem(own + 1, devices)}, device_id_type=mesh_type,
    )
    to_before = pltpu.make_async_remote_copy(
        src_ref=edge_ref.at[pl.ds(0, rim)], dst_ref=after_ref,
        send_sem=rim_sems.at[2], recv_sem=rim_sems.at[3],
        device_id={"mesh": lax.rem(own + devices - 1, devices)}, device_id_type=mesh_type,
    )

    @pl.when(own < devices - 1)
    def _():
        to_next.start()

    @pl.when(own > 0)
    def _():
        to_before.start()

    angles = angle_ref[...]
    cos_ref[...] = jnp.cos(angles)
    sin_ref[...] = jnp.sin(angles)
    own_number = (
        lax.broadcasted_iota(jnp.int32, angles.shape, 0) * block_faces
        + lax.broadcasted_iota(jnp.int32, angles.shape, 1)
    )
    wall_ref[...] = jnp.where(links_ref[...] == own_number, 1.0, 0.0)
    right_ref[...] = jnp.zeros_like(right_ref)
    moved_ref[...] = jnp.zeros_like(moved_ref)
    got_ref[own] = jnp.zeros(got_ref.shape[1:], jnp.float32)

    def volume(pair, right_ref):
        sides = (order_ref[2 * pair], order_ref[2 * pair + 1])
        factors = jnp.concatenate([metric_ref[sides[0]], metric_ref[sides[1]]], axis=1)
        height = fields_ref[pair, 0]
        flow_x = fields_ref[pair, 1]
        flow_y = fields_ref[pair, 2]
        inverse = 1.0 / height
        pressure = 0.5 * gravity * height * height
        speed_x = flow_x * inverse
        speed_y = flow_y * inverse
        cross = flow_x * speed_y
        flux_f = (flow_x, flow_x * speed_x + pressure, cross)
        flux_g = (flow_y, cross, flow_y * speed_y + pressure)
        for comp in range(3):
            span = slice(comp * lanes, (comp + 1) * lanes)
            right_ref[0:rows, span] = factors[0:1] * flux_f[comp] + factors[2:3] * flux_g[comp]
            right_ref[rows : 2 * rows, span] = (
                factors[1:2] * flux_f[comp] + factors[3:4] * flux_g[comp]
            )

    def early_volume(pair, carry):
        volume(pair, right_ref.at[pair])
        return carry

    lax.fori_loop(0, early, early_volume, 0)

    @pl.when(own > 0)
    def _():
        to_next.wait_recv()
        pool_ref[local_faces : local_faces + rim, :] = before_ref[...]

    @pl.when(own < devices - 1)
    def _():
        to_before.wait_recv()
        pool_ref[local_faces + rim : local_faces + 2 * rim, :] = after_ref[...]

    def one_pair(pair, right_ref):
        sides = (order_ref[2 * pair], order_ref[2 * pair + 1])
        for side in range(2):
            for face in range(block_faces):
                picked_ref[side * block_faces + face : side * block_faces + face + 1, :] = pool_ref[
                    pl.ds(map_ref[sides[side], face], 1), :
                ]

        def face_row(ref, face):
            first = ref[pl.ds(sides[0], 1), :]
            second = ref[pl.ds(sides[1], 1), :]
            cells = slice(face * elements, (face + 1) * elements)
            return jnp.concatenate([first[:, cells], second[:, cells]], axis=1)

        for face in range(faces):
            nodes = [int(node) for node in face_nodes[face]]
            for comp in range(3):
                stack_face(
                    fields_ref, pair, comp, nodes, members, node_count,
                    inner_ref.at[face], comp * face_rows,
                )
            height = inner_ref[face, 0:face_rows]
            flow_x = inner_ref[face, face_rows : 2 * face_rows]
            flow_y = inner_ref[face, 2 * face_rows : 3 * face_rows]
            outside = jnp.concatenate(
                [
                    picked_ref[face * elements : (face + 1) * elements],
                    picked_ref[block_faces + face * elements : block_faces + (face + 1) * elements],
                ],
                axis=0,
            ).T
            normal_x = face_row(cos_ref, face)
            normal_y = face_row(sin_ref, face)
            wall = face_row(wall_ref, face) > 0.5
            half_scale = 0.5 * face_row(scale_ref, face)
            flow = flow_x * normal_x + flow_y * normal_y
            out_height = jnp.where(wall, height, outside[0:face_rows])
            out_x = jnp.where(
                wall, flow_x - 2.0 * flow * normal_x, outside[face_rows : 2 * face_rows]
            )
            out_y = jnp.where(
                wall, flow_y - 2.0 * flow * normal_y, outside[2 * face_rows : 3 * face_rows]
            )
            out_flow = out_x * normal_x + out_y * normal_y
            speed = flow / height
            out_speed = out_flow / out_height
            wave = jnp.maximum(
                jnp.abs(speed) + jnp.sqrt(gravity * height),
                jnp.abs(out_speed) + jnp.sqrt(gravity * out_height),
            )
            pressure = 0.5 * gravity * (height * height - out_height * out_height)
            jumps = (
                flow - out_flow + wave * (out_height - height),
                flow_x * speed - out_x * out_speed + pressure * normal_x + wave * (out_x - flow_x),
                flow_y * speed - out_y * out_speed + pressure * normal_y + wave * (out_y - flow_y),
            )
            start = 2 * rows + face * face_rows
            for comp in range(3):
                right_ref[start : start + face_rows, comp * lanes : (comp + 1) * lanes] = (
                    half_scale * jumps[comp]
                )

        right = right_ref[...]
        right_high = right.astype(jnp.bfloat16)
        right_low = (right - right_high.astype(jnp.float32)).astype(jnp.bfloat16)
        high = high_ref[...]
        tendency = (
            jnp.dot(high, right_high, preferred_element_type=jnp.float32)
            + jnp.dot(high, right_low, preferred_element_type=jnp.float32)
            + jnp.dot(
                low_ref[...], right_high[low_start:], preferred_element_type=jnp.float32
            )
        )
        row_low = lanes_low((1, lanes), elements)
        step = time_step * jnp.where(
            row_low, wet_ref[sides[0]].astype(jnp.float32), wet_ref[sides[1]].astype(jnp.float32)
        )

        def inflow(member):
            return breach_rate * jnp.where(
                row_low,
                breach_ref[member, sides[0]].astype(jnp.float32),
                breach_ref[member, sides[1]].astype(jnp.float32),
            )

        def inflow_rows(first, size):
            row_ids = lax.broadcasted_iota(jnp.int32, (size, lanes), 0)
            total = jnp.zeros((size, lanes), jnp.float32)
            for member in range(size):
                total = jnp.where(row_ids == member, inflow(first + member), total)
            return total

        for first, size in ((0, full), (full, rest)):
            source = inflow_rows(first, size)
            low = lanes_low((size, lanes), elements)
            for comp in range(3):
                span = slice(comp * lanes, (comp + 1) * lanes)
                for half in range(node_count // 2):
                    both = []
                    for side in range(2):
                        base = node_count * first + (2 * half + side) * size
                        change = tendency[base : base + size, span]
                        if comp == 0:
                            change = change + source
                        both.append(fields_ref[pair, comp, base : base + size, :] + step * change)
                    one = jnp.where(low, both[0], pltpu.roll(both[1], elements, 1))
                    two = jnp.where(low, pltpu.roll(both[0], elements, 1), both[1])
                    base = halves * 3 * first + (comp * halves + half) * size
                    moved_ref[2 * pair, base : base + size, :] = one
                    moved_ref[2 * pair + 1, base : base + size, :] = two


    def early_pair(pair, carry):
        one_pair(pair, right_ref.at[pair])
        return carry

    def late_pair(pair, carry):
        volume(pair, right_ref.at[0])
        one_pair(pair, right_ref.at[0])
        return carry

    lax.fori_loop(0, early, early_pair, 0)

    def one_send(device, carry):
        send_ref[device] = moved_ref[chosen_ref[device]]
        return carry

    lax.fori_loop(0, devices, one_send, 0)
    sends = []
    for step in sorted(range(1, devices), key=lambda step: abs(step - devices // 2)):
        target = lax.rem(own + step, devices)
        sends.append(
            pltpu.make_async_remote_copy(
                src_ref=send_ref.at[target], dst_ref=got_ref.at[own],
                send_sem=send_sems.at[target], recv_sem=got_sems.at[own],
                device_id={"mesh": target}, device_id_type=mesh_type,
            )
        )
    for copy in sends:
        copy.start()

    lax.fori_loop(early, blocks // 2, late_pair, 0)

    for step in range(1, devices):
        origin = lax.rem(own + step, devices)
        pltpu.make_async_remote_copy(
            src_ref=send_ref.at[origin], dst_ref=got_ref.at[origin],
            send_sem=send_sems.at[origin], recv_sem=got_sems.at[origin],
            device_id={"mesh": origin}, device_id_type=mesh_type,
        ).wait_recv()

    def one_slot(slot, carry):
        stays = source_ref[slot] == own
        block = jnp.where(stays, moved_ref[slot_ref[slot]], got_ref[source_ref[slot]])
        for comp in range(3):
            for half in range(halves):
                for first, size in ((0, full), (full, rest)):
                    base = halves * 3 * first + (comp * halves + half) * size
                    value = block[base : base + size]
                    cells = (slice(first, first + size), slice(half * lanes, (half + 1) * lanes))
                    if comp == 0:
                        depth_out[(slot, *cells)] = value
                    else:
                        flow_out[(slot, comp - 1, *cells)] = value
        return carry

    lax.fori_loop(0, blocks, one_slot, 0)
    for copy in sends:
        copy.wait_send()

    @pl.when(own < devices - 1)
    def _():
        to_next.wait_send()

    @pl.when(own > 0)
    def _():
        to_before.wait_send()


def body(
    water_depth,
    momentum,
    metric,
    face_scale,
    face_angle,
    face_map,
    rim_faces,
    wet_blocks,
    breach,
    block_plan,
):
    face_nodes = node_tables()[3]
    node_count = int(face_nodes.max()) + 1
    blocks, members, node_cells = water_depth.shape
    elements = node_cells // node_count
    lanes = 2 * elements
    rows = round_up(node_count * members, 16)
    block_faces = faces * elements
    local_faces = blocks * block_faces
    rim_count = rim_faces.shape[1]
    rim = rim_count // 2
    own = lax.axis_index("mesh").astype(jnp.int32)
    devices = lax.axis_size("mesh")
    f32 = jnp.float32

    local_ids = jnp.arange(blocks, dtype=jnp.int32)
    targets = lax.dynamic_slice_in_dim(block_plan, own * blocks, blocks) // blocks
    stays = (targets == own).astype(jnp.int32)
    keys = stays * blocks + local_ids
    place = jnp.sum((keys[None, :] < keys[:, None]).astype(jnp.int32), axis=1)
    order = jnp.sum(jnp.where(place[None, :] == local_ids[:, None], local_ids[None, :], 0), axis=1)
    device_ids = jnp.arange(devices, dtype=jnp.int32)
    chosen = jnp.sum(jnp.where(targets[None, :] == device_ids[:, None], place[None, :], 0), axis=1)
    chosen = jnp.where(device_ids == own, 0, chosen)
    slot_ids = own * blocks + local_ids
    every_slot = jnp.arange(block_plan.shape[0], dtype=jnp.int32)
    source = jnp.sum(
        jnp.where(block_plan[None, :] == slot_ids[:, None], every_slot[None, :], 0), axis=1
    )
    origin = jnp.clip(source - own * blocks, 0, blocks - 1)
    slot_place = jnp.sum(jnp.where(origin[:, None] == local_ids[None, :], place[None, :], 0), axis=1)
    source = source // blocks

    owner = face_map // block_faces
    shifts = (place - local_ids) * block_faces
    links = face_map + jnp.sum(
        jnp.where(owner[None] == local_ids[:, None, None], shifts[:, None, None], 0), axis=0
    )

    high, low = combined_matrix(members, rows, node_count)
    low_start = 2 * rows if not np.any(low[:, : 2 * rows].astype(np.float32)) else 0
    early = min(-(-(devices // 2) // 2), blocks // 2)
    block_rows = round_up(3 * members * (node_count // 2), 8)
    return pl.pallas_call(
        lambda *refs: section_kernel(face_nodes, node_count, members, low_start, early, *refs),
        out_shape=(
            jax.ShapeDtypeStruct(water_depth.shape, f32),
            jax.ShapeDtypeStruct(momentum.shape, f32),
        ),
        in_specs=[SMEM] * 9 + [VMEM] * 8,
        out_specs=(VMEM, VMEM),
        scratch_shapes=[
            pltpu.VMEM((blocks // 2, 3, rows, lanes), f32),
            pltpu.VMEM((local_faces + rim_count, lanes), f32),
            pltpu.VMEM((rim_count, lanes), f32),
            pltpu.VMEM((rim, lanes), f32),
            pltpu.VMEM((rim, lanes), f32),
            pltpu.VMEM((2 * block_faces, lanes), f32),
            pltpu.VMEM((faces, lanes, lanes), f32),
            pltpu.VMEM((blocks, block_faces), f32),
            pltpu.VMEM((blocks, block_faces), f32),
            pltpu.VMEM((blocks, block_faces), f32),
            pltpu.VMEM((early, high.shape[1], 3 * lanes), f32),
            pltpu.VMEM((blocks, block_rows, lanes), f32),
            pltpu.VMEM((devices, block_rows, lanes), f32),
            pltpu.VMEM((devices, block_rows, lanes), f32),
            pltpu.SemaphoreType.DMA((4,)),
            pltpu.SemaphoreType.DMA((devices,)),
            pltpu.SemaphoreType.DMA((devices,)),
        ],
        compiler_params=pltpu.CompilerParams(
            vmem_limit_bytes=48 * 2**20, collective_id=0, has_side_effects=True
        ),
    )(
        order, place, links, rim_faces, wet_blocks, breach.T, chosen,
        slot_place, source, water_depth, momentum, metric, face_scale, face_angle, face_map,
        jnp.asarray(high), jnp.asarray(low[:, low_start:]),
    )


def solution(mesh):
    in_specs = (
        P(("groups", "mesh"), None, None),
        P(("groups", "mesh"), None, None, None),
        P(("groups", "mesh"), None, None),
        P(("groups", "mesh"), None),
        P(("groups", "mesh"), None),
        P(("groups", "mesh"), None),
        P(("groups", "mesh"), None),
        P(("groups", "mesh")),
        P(("groups", "mesh"), None),
        P("groups"),
    )
    out_specs = (P(("groups", "mesh"), None, None), P(("groups", "mesh"), None, None, None))
    return jax.shard_map(body, mesh=mesh, in_specs=in_specs, out_specs=out_specs, check_vma=False)
```

```python
import math

import jax
import jax.numpy as jnp
import numpy as np
import ml_dtypes
from jax import lax
from jax.experimental import pallas as pl
from jax.experimental.pallas import tpu as pltpu
from jax.sharding import PartitionSpec as P

time_step = 0.01
gravity = 1.0
breach_rate = 5.0


SMEM = pl.BlockSpec(memory_space=pltpu.SMEM)
VMEM = pl.BlockSpec(memory_space=pltpu.VMEM)
ANY = pl.BlockSpec(memory_space=pl.ANY)
faces, face_points = 3, 4


def gauss_solve(matrix, right):
    dimension = matrix.shape[0]
    augmented = np.concatenate([np.array(matrix) * 1.0, np.array(right) * 1.0], axis=1)
    for pivot_col in range(dimension):
        largest = pivot_col + int(np.argmax(np.abs(augmented[pivot_col:, pivot_col])))
        swapped = augmented[[largest, pivot_col]]
        augmented[[pivot_col, largest]] = swapped
        augmented[pivot_col] = augmented[pivot_col] / augmented[pivot_col, pivot_col]
        for row_id in range(dimension):
            if row_id != pivot_col:
                augmented[row_id] = (
                    augmented[row_id] - augmented[row_id, pivot_col] * augmented[pivot_col]
                )
    return augmented[:, dimension:]


def node_tables():
    points = np.array(
        [(across / 3.0, upward / 3.0) for upward in range(4) for across in range(4 - upward)]
    )
    powers = [(power_r, power_s) for power_r in range(4) for power_s in range(4 - power_r)]
    vander = np.zeros((10, 10))
    grad_r = np.zeros((10, 10))
    grad_s = np.zeros((10, 10))
    mono_mass = np.zeros((10, 10))
    for column, (power_r, power_s) in enumerate(powers):
        vander[:, column] = points[:, 0] ** power_r * points[:, 1] ** power_s
        if power_r > 0:
            grad_r[:, column] = power_r * points[:, 0] ** (power_r - 1) * points[:, 1] ** power_s
        if power_s > 0:
            grad_s[:, column] = power_s * points[:, 0] ** power_r * points[:, 1] ** (power_s - 1)
        for second_column, (other_r, other_s) in enumerate(powers):
            mono_mass[column, second_column] = (
                math.factorial(power_r + other_r)
                * math.factorial(power_s + other_s)
                / math.factorial(power_r + other_r + power_s + other_s + 2)
            )
    inverse = gauss_solve(vander, np.eye(10))
    mass_matrix = inverse.T @ mono_mass @ inverse
    line_points = np.arange(4) / 3.0
    line_vander = line_points[:, None] ** np.arange(4)[None, :]
    hilbert = 1.0 / (np.arange(4)[:, None] + np.arange(4)[None, :] + 1.0)
    line_inverse = gauss_solve(line_vander, np.eye(4))
    edge_mass = line_inverse.T @ hilbert @ line_inverse
    face_nodes = np.array([[0, 1, 2, 3], [3, 6, 8, 9], [9, 7, 4, 0]])
    edge_embed = np.zeros((10, 12))
    for face_id in range(3):
        for node_id in range(4):
            edge_embed[face_nodes[face_id, node_id], 4 * face_id : 4 * face_id + 4] += edge_mass[
                node_id
            ]
    lifting = gauss_solve(mass_matrix, edge_embed).reshape(10, 3, 4)
    return (
        np.asarray(grad_r @ inverse, np.float32),
        np.asarray(grad_s @ inverse, np.float32),
        np.asarray(lifting, np.float32),
        face_nodes,
    )


def round_up(count, step):
    return -(-count // step) * step


def combined_matrix(members, rows, node_count):
    deriv_r, deriv_s, lifting, _ = node_tables()
    full = members // 8 * 8
    rest = members - full
    face_rows = face_points * members
    columns = 2 * rows + round_up(faces * face_rows, 16)

    def place(point, member, points):
        if member < full:
            return point * full + member
        return points * full + point * rest + member - full

    table = np.zeros((rows, columns), np.float32)
    for member in range(members):
        for node in range(node_count):
            row = place(node, member, node_count)
            for other in range(node_count):
                column = place(other, member, node_count)
                table[row, column] = -deriv_r[node, other]
                table[row, rows + column] = -deriv_s[node, other]
            for face in range(faces):
                for point in range(face_points):
                    column = 2 * rows + face * face_rows + place(point, member, face_points)
                    table[row, column] = lifting[node, face, point]
    high = table.astype(ml_dtypes.bfloat16)
    low = (table - high.astype(np.float32)).astype(ml_dtypes.bfloat16)
    return high, low


def lanes_low(shape, elements):
    return lax.broadcasted_iota(jnp.int32, shape, len(shape) - 1) < elements


def stack_face(fields_ref, pair, comp, nodes, members, node_count, out_ref, start):
    full = members // 8 * 8
    rest = members - full
    for point, node in enumerate(nodes):
        out_ref[start + point * full : start + (point + 1) * full, :] = fields_ref[
            pair, comp, node * full : (node + 1) * full, :
        ]
    base = node_count * full
    tail = start + len(nodes) * full
    for point, node in enumerate(nodes):
        out_ref[tail + point * rest : tail + (point + 1) * rest, :] = fields_ref[
            pair, comp, base + node * rest : base + (node + 1) * rest, :
        ]


def lay_out(pair, sides, node_count, depth_ref, flow_ref, fields_ref):
    members, node_cells = depth_ref.shape[1:]
    elements = node_cells // node_count
    lanes = 2 * elements
    full = members // 8 * 8
    rest = members - full
    used = node_count * members
    rows = fields_ref.shape[2]
    for comp in range(3):
        fields_ref[pair, comp, used:rows, :] = jnp.ones((rows - used, lanes), jnp.float32)
        for half in range(node_count // 2):
            for first, size in ((0, full), (full, rest)):
                cells = (pl.ds(first, size), pl.ds(half * lanes, lanes))
                if comp == 0:
                    one = depth_ref[(sides[0], *cells)]
                    two = depth_ref[(sides[1], *cells)]
                else:
                    one = flow_ref[(sides[0], comp - 1, *cells)]
                    two = flow_ref[(sides[1], comp - 1, *cells)]
                low = lanes_low(one.shape, elements)
                base = node_count * first + 2 * half * size
                fields_ref[pair, comp, base : base + size, :] = jnp.where(
                    low, one, pltpu.roll(two, elements, 1)
                )
                fields_ref[pair, comp, base + size : base + 2 * size, :] = jnp.where(
                    low, pltpu.roll(one, elements, 1), two
                )


def make_table(
    face_nodes, node_count, depth_ref, flow_ref, rim_ref, fields_ref, table_ref, edge_ref, stack_ref
):
    blocks, members, node_cells = depth_ref.shape
    elements = node_cells // node_count
    face_rows = face_points * members
    stack_ref[...] = jnp.zeros_like(stack_ref)
    for pair in range(blocks // 2):
        lay_out(pair, (2 * pair, 2 * pair + 1), node_count, depth_ref, flow_ref, fields_ref)
        for face in range(faces):
            nodes = [int(node) for node in face_nodes[face][::-1]]
            stacked = stack_ref.at[pair % 2, face]
            for comp in range(3):
                stack_face(
                    fields_ref, pair, comp, nodes, members, node_count, stacked, comp * face_rows
                )
            turned = stacked[...].T
            for side in range(2):
                start = ((2 * pair + side) * faces + face) * elements
                table_ref[start : start + elements, :] = (
                    turned[side * elements : (side + 1) * elements]
                )

    def one_group(group, carry):
        for step in range(16):
            face = group * 16 + step
            edge_ref[pl.ds(face, 1), :] = table_ref[pl.ds(rim_ref[0, face], 1), :]
        return carry

    lax.fori_loop(0, rim_ref.shape[1] // 16, one_group, 0)


def section_kernel(
    face_nodes, node_count, members, low_start, early,
    order_ref, map_ref, rim_ref, wet_ref, breach_ref, chosen_ref, slot_ref, source_ref,
    depth_ref, flow_ref, metric_ref, scale_ref, angle_ref, links_ref, high_ref, low_ref,
    depth_out, flow_out,
    natural_ref, fields_ref, pool_ref, edge_ref, before_ref, after_ref, picked_ref, inner_ref,
    cos_ref, sin_ref, wall_ref, right_ref, moved_ref, send_ref, got_ref,
    rim_sems, send_sems, got_sems,
):
    blocks = depth_out.shape[0]
    elements = metric_ref.shape[2]
    lanes = 2 * elements
    rows = fields_ref.shape[2]
    full = members // 8 * 8
    rest = members - full
    face_rows = face_points * members
    halves = node_count // 2
    block_faces = faces * elements
    local_faces = blocks * block_faces
    rim = before_ref.shape[0]
    devices = got_ref.shape[0]
    own = lax.axis_index("mesh")
    mesh_type = pl.DeviceIdType.MESH

    barrier = pltpu.get_barrier_semaphore()
    for step in range(1, devices):
        pl.semaphore_signal(
            barrier, inc=1, device_id={"mesh": lax.rem(own + step, devices)},
            device_id_type=mesh_type,
        )

    make_table(
        face_nodes, node_count, depth_ref, flow_ref, rim_ref,
        natural_ref, pool_ref, edge_ref, inner_ref,
    )
    pl.semaphore_wait(barrier, devices - 1)

    to_next = pltpu.make_async_remote_copy(
        src_ref=edge_ref.at[pl.ds(rim, rim)], dst_ref=before_ref,
        send_sem=rim_sems.at[0], recv_sem=rim_sems.at[1],
        device_id={"mesh": lax.rem(own + 1, devices)}, device_id_type=mesh_type,
    )
    to_before = pltpu.make_async_remote_copy(
        src_ref=edge_ref.at[pl.ds(0, rim)], dst_ref=after_ref,
        send_sem=rim_sems.at[2], recv_sem=rim_sems.at[3],
        device_id={"mesh": lax.rem(own + devices - 1, devices)}, device_id_type=mesh_type,
    )

    @pl.when(own < devices - 1)
    def _():
        to_next.start()

    @pl.when(own > 0)
    def _():
        to_before.start()

    angles = angle_ref[...]
    cos_ref[...] = jnp.cos(angles)
    sin_ref[...] = jnp.sin(angles)
    own_number = (
        lax.broadcasted_iota(jnp.int32, angles.shape, 0) * block_faces
        + lax.broadcasted_iota(jnp.int32, angles.shape, 1)
    )
    wall_ref[...] = jnp.where(links_ref[...] == own_number, 1.0, 0.0)
    right_ref[...] = jnp.zeros_like(right_ref)
    moved_ref[...] = jnp.zeros_like(moved_ref)
    got_ref[own] = jnp.zeros(got_ref.shape[1:], jnp.float32)

    def volume(pair, right_ref):
        sides = (order_ref[2 * pair], order_ref[2 * pair + 1])
        lay_out(pair, sides, node_count, depth_ref, flow_ref, fields_ref)
        factors = jnp.concatenate([metric_ref[sides[0]], metric_ref[sides[1]]], axis=1)
        height = fields_ref[pair, 0]
        flow_x = fields_ref[pair, 1]
        flow_y = fields_ref[pair, 2]
        inverse = 1.0 / height
        pressure = 0.5 * gravity * height * height
        speed_x = flow_x * inverse
        speed_y = flow_y * inverse
        cross = flow_x * speed_y
        flux_f = (flow_x, flow_x * speed_x + pressure, cross)
        flux_g = (flow_y, cross, flow_y * speed_y + pressure)
        for comp in range(3):
            span = slice(comp * lanes, (comp + 1) * lanes)
            right_ref[0:rows, span] = factors[0:1] * flux_f[comp] + factors[2:3] * flux_g[comp]
            right_ref[rows : 2 * rows, span] = (
                factors[1:2] * flux_f[comp] + factors[3:4] * flux_g[comp]
            )

    for pair in range(early):
        volume(pair, right_ref.at[pair])

    @pl.when(own > 0)
    def _():
        to_next.wait_recv()
        pool_ref[local_faces : local_faces + rim, :] = before_ref[...]

    @pl.when(own < devices - 1)
    def _():
        to_before.wait_recv()
        pool_ref[local_faces + rim : local_faces + 2 * rim, :] = after_ref[...]

    def one_pair(pair, right_ref, picked_ref, inner_ref):
        sides = (order_ref[2 * pair], order_ref[2 * pair + 1])
        for side in range(2):
            for face in range(block_faces):
                picked_ref[side * block_faces + face : side * block_faces + face + 1, :] = pool_ref[
                    pl.ds(map_ref[sides[side], face], 1), :
                ]

        def face_row(ref, face):
            first = ref[pl.ds(sides[0], 1), :]
            second = ref[pl.ds(sides[1], 1), :]
            cells = slice(face * elements, (face + 1) * elements)
            return jnp.concatenate([first[:, cells], second[:, cells]], axis=1)

        for face in range(faces):
            nodes = [int(node) for node in face_nodes[face]]
            for comp in range(3):
                stack_face(
                    fields_ref, pair, comp, nodes, members, node_count,
                    inner_ref.at[face], comp * face_rows,
                )
            height = inner_ref[face, 0:face_rows]
            flow_x = inner_ref[face, face_rows : 2 * face_rows]
            flow_y = inner_ref[face, 2 * face_rows : 3 * face_rows]
            outside = jnp.concatenate(
                [
                    picked_ref[face * elements : (face + 1) * elements],
                    picked_ref[block_faces + face * elements : block_faces + (face + 1) * elements],
                ],
                axis=0,
            ).T
            normal_x = face_row(cos_ref, face)
            normal_y = face_row(sin_ref, face)
            wall = face_row(wall_ref, face) > 0.5
            half_scale = 0.5 * face_row(scale_ref, face)
            flow = flow_x * normal_x + flow_y * normal_y
            out_height = jnp.where(wall, height, outside[0:face_rows])
            out_x = jnp.where(
                wall, flow_x - 2.0 * flow * normal_x, outside[face_rows : 2 * face_rows]
            )
            out_y = jnp.where(
                wall, flow_y - 2.0 * flow * normal_y, outside[2 * face_rows : 3 * face_rows]
            )
            out_flow = out_x * normal_x + out_y * normal_y
            speed = flow / height
            out_speed = out_flow / out_height
            wave = jnp.maximum(
                jnp.abs(speed) + jnp.sqrt(gravity * height),
                jnp.abs(out_speed) + jnp.sqrt(gravity * out_height),
            )
            pressure = 0.5 * gravity * (height * height - out_height * out_height)
            jumps = (
                flow - out_flow + wave * (out_height - height),
                flow_x * speed - out_x * out_speed + pressure * normal_x + wave * (out_x - flow_x),
                flow_y * speed - out_y * out_speed + pressure * normal_y + wave * (out_y - flow_y),
            )
            start = 2 * rows + face * face_rows
            for comp in range(3):
                right_ref[start : start + face_rows, comp * lanes : (comp + 1) * lanes] = (
                    half_scale * jumps[comp]
                )

        right = right_ref[...]
        right_high = right.astype(jnp.bfloat16)
        right_low = (right - right_high.astype(jnp.float32)).astype(jnp.bfloat16)
        high = high_ref[...]
        tendency = (
            jnp.dot(high, right_high, preferred_element_type=jnp.float32)
            + jnp.dot(high, right_low, preferred_element_type=jnp.float32)
            + jnp.dot(
                low_ref[...], right_high[low_start:], preferred_element_type=jnp.float32
            )
        )
        row_low = lanes_low((1, lanes), elements)
        step = time_step * jnp.where(
            row_low, wet_ref[sides[0]].astype(jnp.float32), wet_ref[sides[1]].astype(jnp.float32)
        )

        def inflow(member):
            return breach_rate * jnp.where(
                row_low,
                breach_ref[member, sides[0]].astype(jnp.float32),
                breach_ref[member, sides[1]].astype(jnp.float32),
            )

        def inflow_rows(first, size):
            row_ids = lax.broadcasted_iota(jnp.int32, (size, lanes), 0)
            total = jnp.zeros((size, lanes), jnp.float32)
            for member in range(size):
                total = jnp.where(row_ids == member, inflow(first + member), total)
            return total

        for first, size in ((0, full), (full, rest)):
            source = inflow_rows(first, size)
            low = lanes_low((size, lanes), elements)
            for comp in range(3):
                span = slice(comp * lanes, (comp + 1) * lanes)
                for half in range(node_count // 2):
                    both = []
                    for side in range(2):
                        base = node_count * first + (2 * half + side) * size
                        change = tendency[base : base + size, span]
                        if comp == 0:
                            change = change + source
                        both.append(fields_ref[pair, comp, base : base + size, :] + step * change)
                    one = jnp.where(low, both[0], pltpu.roll(both[1], elements, 1))
                    two = jnp.where(low, pltpu.roll(both[0], elements, 1), both[1])
                    base = halves * 3 * first + (comp * halves + half) * size
                    moved_ref[2 * pair, base : base + size, :] = one
                    moved_ref[2 * pair + 1, base : base + size, :] = two


    def late_pair(pair, carry):
        volume(pair, right_ref.at[0])
        one_pair(pair, right_ref.at[0], picked_ref.at[0], inner_ref.at[0])
        return carry

    for pair in range(early):
        one_pair(pair, right_ref.at[pair], picked_ref.at[pair % 2], inner_ref.at[pair % 2])

    def one_send(device, carry):
        send_ref[device] = moved_ref[chosen_ref[device]]
        return carry

    lax.fori_loop(0, devices, one_send, 0)
    sends = []
    half_devices = devices // 2
    own_half = own // half_devices
    for step in [*range(half_devices, devices), *range(1, half_devices)]:
        side = own_half if step < half_devices else 1 - own_half
        target = side * half_devices + lax.rem(own + step, half_devices)
        sends.append(
            pltpu.make_async_remote_copy(
                src_ref=send_ref.at[target], dst_ref=got_ref.at[own],
                send_sem=send_sems.at[target], recv_sem=got_sems.at[own],
                device_id={"mesh": target}, device_id_type=mesh_type,
            )
        )
    for copy in sends:
        copy.start()

    lax.fori_loop(early, blocks // 2, late_pair, 0)

    for step in range(1, devices):
        origin = lax.rem(own + step, devices)
        pltpu.make_async_remote_copy(
            src_ref=send_ref.at[origin], dst_ref=got_ref.at[origin],
            send_sem=send_sems.at[origin], recv_sem=got_sems.at[origin],
            device_id={"mesh": origin}, device_id_type=mesh_type,
        ).wait_recv()

    def one_slot(slot, carry):
        stays = source_ref[slot] == own
        block = jnp.where(stays, moved_ref[slot_ref[slot]], got_ref[source_ref[slot]])
        for comp in range(3):
            for half in range(halves):
                for first, size in ((0, full), (full, rest)):
                    base = halves * 3 * first + (comp * halves + half) * size
                    value = block[base : base + size]
                    cells = (slice(first, first + size), slice(half * lanes, (half + 1) * lanes))
                    if comp == 0:
                        depth_out[(slot, *cells)] = value
                    else:
                        flow_out[(slot, comp - 1, *cells)] = value
        return carry

    lax.fori_loop(0, blocks, one_slot, 0)
    for copy in sends:
        copy.wait_send()

    @pl.when(own < devices - 1)
    def _():
        to_next.wait_send()

    @pl.when(own > 0)
    def _():
        to_before.wait_send()


def body(
    water_depth,
    momentum,
    metric,
    face_scale,
    face_angle,
    face_map,
    rim_faces,
    wet_blocks,
    breach,
    block_plan,
):
    face_nodes = node_tables()[3]
    node_count = int(face_nodes.max()) + 1
    blocks, members, node_cells = water_depth.shape
    elements = node_cells // node_count
    lanes = 2 * elements
    rows = round_up(node_count * members, 16)
    block_faces = faces * elements
    local_faces = blocks * block_faces
    rim_count = rim_faces.shape[1]
    rim = rim_count // 2
    own = lax.axis_index("mesh").astype(jnp.int32)
    devices = lax.axis_size("mesh")
    f32 = jnp.float32

    local_ids = jnp.arange(blocks, dtype=jnp.int32)
    targets = lax.dynamic_slice_in_dim(block_plan, own * blocks, blocks) // blocks
    stays = (targets == own).astype(jnp.int32)
    keys = stays * blocks + local_ids
    place = jnp.sum((keys[None, :] < keys[:, None]).astype(jnp.int32), axis=1)
    order = jnp.sum(jnp.where(place[None, :] == local_ids[:, None], local_ids[None, :], 0), axis=1)
    device_ids = jnp.arange(devices, dtype=jnp.int32)
    chosen = jnp.sum(jnp.where(targets[None, :] == device_ids[:, None], place[None, :], 0), axis=1)
    chosen = jnp.where(device_ids == own, 0, chosen)
    slot_ids = own * blocks + local_ids
    every_slot = jnp.arange(block_plan.shape[0], dtype=jnp.int32)
    source = jnp.sum(
        jnp.where(block_plan[None, :] == slot_ids[:, None], every_slot[None, :], 0), axis=1
    )
    origin = jnp.clip(source - own * blocks, 0, blocks - 1)
    slot_place = jnp.sum(jnp.where(origin[:, None] == local_ids[None, :], place[None, :], 0), axis=1)
    source = source // blocks

    high, low = combined_matrix(members, rows, node_count)
    low_start = 2 * rows if not np.any(low[:, : 2 * rows].astype(np.float32)) else 0
    early = min(-(-(devices // 2) // 2), blocks // 2)
    block_rows = round_up(3 * members * (node_count // 2), 8)
    return pl.pallas_call(
        lambda *refs: section_kernel(face_nodes, node_count, members, low_start, early, *refs),
        out_shape=(
            jax.ShapeDtypeStruct(water_depth.shape, f32),
            jax.ShapeDtypeStruct(momentum.shape, f32),
        ),
        in_specs=[SMEM] * 8 + [VMEM] * 8,
        out_specs=(VMEM, VMEM),
        scratch_shapes=[
            pltpu.VMEM((blocks // 2, 3, rows, lanes), f32),
            pltpu.VMEM((blocks // 2, 3, rows, lanes), f32),
            pltpu.VMEM((local_faces + rim_count, lanes), f32),
            pltpu.VMEM((rim_count, lanes), f32),
            pltpu.VMEM((rim, lanes), f32),
            pltpu.VMEM((rim, lanes), f32),
            pltpu.VMEM((2, 2 * block_faces, lanes), f32),
            pltpu.VMEM((2, faces, lanes, lanes), f32),
            pltpu.VMEM((blocks, block_faces), f32),
            pltpu.VMEM((blocks, block_faces), f32),
            pltpu.VMEM((blocks, block_faces), f32),
            pltpu.VMEM((early, high.shape[1], 3 * lanes), f32),
            pltpu.VMEM((blocks, block_rows, lanes), f32),
            pltpu.VMEM((devices, block_rows, lanes), f32),
            pltpu.VMEM((devices, block_rows, lanes), f32),
            pltpu.SemaphoreType.DMA((4,)),
            pltpu.SemaphoreType.DMA((devices,)),
            pltpu.SemaphoreType.DMA((devices,)),
        ],
        compiler_params=pltpu.CompilerParams(
            vmem_limit_bytes=48 * 2**20, collective_id=0, has_side_effects=True
        ),
    )(
        order, face_map, rim_faces, wet_blocks, breach.T, chosen,
        slot_place, source, water_depth, momentum, metric, face_scale, face_angle, face_map,
        jnp.asarray(high), jnp.asarray(low[:, low_start:]),
    )


def solution(mesh):
    in_specs = (
        P(("groups", "mesh"), None, None),
        P(("groups", "mesh"), None, None, None),
        P(("groups", "mesh"), None, None),
        P(("groups", "mesh"), None),
        P(("groups", "mesh"), None),
        P(("groups", "mesh"), None),
        P(("groups", "mesh"), None),
        P(("groups", "mesh")),
        P(("groups", "mesh"), None),
        P("groups"),
    )
    out_specs = (P(("groups", "mesh"), None, None), P(("groups", "mesh"), None, None, None))
    return jax.shard_map(body, mesh=mesh, in_specs=in_specs, out_specs=out_specs, check_vma=False)
```

```python
import math

import jax
import jax.numpy as jnp
import numpy as np
import ml_dtypes
from jax import lax
from jax.experimental import pallas as pl
from jax.experimental.pallas import tpu as pltpu
from jax.sharding import PartitionSpec as P

time_step = 0.01
gravity = 1.0
breach_rate = 5.0


SMEM = pl.BlockSpec(memory_space=pltpu.SMEM)
VMEM = pl.BlockSpec(memory_space=pltpu.VMEM)
ANY = pl.BlockSpec(memory_space=pl.ANY)
faces, face_points = 3, 4


def gauss_solve(matrix, right):
    dimension = matrix.shape[0]
    augmented = np.concatenate([np.array(matrix) * 1.0, np.array(right) * 1.0], axis=1)
    for pivot_col in range(dimension):
        largest = pivot_col + int(np.argmax(np.abs(augmented[pivot_col:, pivot_col])))
        swapped = augmented[[largest, pivot_col]]
        augmented[[pivot_col, largest]] = swapped
        augmented[pivot_col] = augmented[pivot_col] / augmented[pivot_col, pivot_col]
        for row_id in range(dimension):
            if row_id != pivot_col:
                augmented[row_id] = (
                    augmented[row_id] - augmented[row_id, pivot_col] * augmented[pivot_col]
                )
    return augmented[:, dimension:]


def node_tables():
    points = np.array(
        [(across / 3.0, upward / 3.0) for upward in range(4) for across in range(4 - upward)]
    )
    powers = [(power_r, power_s) for power_r in range(4) for power_s in range(4 - power_r)]
    vander = np.zeros((10, 10))
    grad_r = np.zeros((10, 10))
    grad_s = np.zeros((10, 10))
    mono_mass = np.zeros((10, 10))
    for column, (power_r, power_s) in enumerate(powers):
        vander[:, column] = points[:, 0] ** power_r * points[:, 1] ** power_s
        if power_r > 0:
            grad_r[:, column] = power_r * points[:, 0] ** (power_r - 1) * points[:, 1] ** power_s
        if power_s > 0:
            grad_s[:, column] = power_s * points[:, 0] ** power_r * points[:, 1] ** (power_s - 1)
        for second_column, (other_r, other_s) in enumerate(powers):
            mono_mass[column, second_column] = (
                math.factorial(power_r + other_r)
                * math.factorial(power_s + other_s)
                / math.factorial(power_r + other_r + power_s + other_s + 2)
            )
    inverse = gauss_solve(vander, np.eye(10))
    mass_matrix = inverse.T @ mono_mass @ inverse
    line_points = np.arange(4) / 3.0
    line_vander = line_points[:, None] ** np.arange(4)[None, :]
    hilbert = 1.0 / (np.arange(4)[:, None] + np.arange(4)[None, :] + 1.0)
    line_inverse = gauss_solve(line_vander, np.eye(4))
    edge_mass = line_inverse.T @ hilbert @ line_inverse
    face_nodes = np.array([[0, 1, 2, 3], [3, 6, 8, 9], [9, 7, 4, 0]])
    edge_embed = np.zeros((10, 12))
    for face_id in range(3):
        for node_id in range(4):
            edge_embed[face_nodes[face_id, node_id], 4 * face_id : 4 * face_id + 4] += edge_mass[
                node_id
            ]
    lifting = gauss_solve(mass_matrix, edge_embed).reshape(10, 3, 4)
    return (
        np.asarray(grad_r @ inverse, np.float32),
        np.asarray(grad_s @ inverse, np.float32),
        np.asarray(lifting, np.float32),
        face_nodes,
    )


def round_up(count, step):
    return -(-count // step) * step


def combined_matrix(members, rows, node_count):
    deriv_r, deriv_s, lifting, _ = node_tables()
    full = members // 8 * 8
    rest = members - full
    face_rows = face_points * members
    columns = 2 * rows + round_up(faces * face_rows, 16)

    def place(point, member, points):
        if member < full:
            return point * full + member
        return points * full + point * rest + member - full

    table = np.zeros((rows, columns), np.float32)
    for member in range(members):
        for node in range(node_count):
            row = place(node, member, node_count)
            for other in range(node_count):
                column = place(other, member, node_count)
                table[row, column] = -deriv_r[node, other]
                table[row, rows + column] = -deriv_s[node, other]
            for face in range(faces):
                for point in range(face_points):
                    column = 2 * rows + face * face_rows + place(point, member, face_points)
                    table[row, column] = lifting[node, face, point]
    high = table.astype(ml_dtypes.bfloat16)
    low = (table - high.astype(np.float32)).astype(ml_dtypes.bfloat16)
    return high, low


def lanes_low(shape, elements):
    return lax.broadcasted_iota(jnp.int32, shape, len(shape) - 1) < elements


def stack_face(fields_ref, pair, comp, nodes, members, node_count, out_ref, start):
    full = members // 8 * 8
    rest = members - full
    for point, node in enumerate(nodes):
        out_ref[start + point * full : start + (point + 1) * full, :] = fields_ref[
            pair, comp, node * full : (node + 1) * full, :
        ]
    base = node_count * full
    tail = start + len(nodes) * full
    for point, node in enumerate(nodes):
        out_ref[tail + point * rest : tail + (point + 1) * rest, :] = fields_ref[
            pair, comp, base + node * rest : base + (node + 1) * rest, :
        ]


def lay_out(pair, sides, node_count, depth_ref, flow_ref, fields_ref):
    members, node_cells = depth_ref.shape[1:]
    elements = node_cells // node_count
    lanes = 2 * elements
    full = members // 8 * 8
    rest = members - full
    used = node_count * members
    rows = fields_ref.shape[2]
    for comp in range(3):
        fields_ref[pair, comp, used:rows, :] = jnp.ones((rows - used, lanes), jnp.float32)
        for half in range(node_count // 2):
            for first, size in ((0, full), (full, rest)):
                cells = (pl.ds(first, size), pl.ds(half * lanes, lanes))
                if comp == 0:
                    one = depth_ref[(sides[0], *cells)]
                    two = depth_ref[(sides[1], *cells)]
                else:
                    one = flow_ref[(sides[0], comp - 1, *cells)]
                    two = flow_ref[(sides[1], comp - 1, *cells)]
                low = lanes_low(one.shape, elements)
                base = node_count * first + 2 * half * size
                fields_ref[pair, comp, base : base + size, :] = jnp.where(
                    low, one, pltpu.roll(two, elements, 1)
                )
                fields_ref[pair, comp, base + size : base + 2 * size, :] = jnp.where(
                    low, pltpu.roll(one, elements, 1), two
                )


def make_table(
    face_nodes, node_count, depth_ref, flow_ref, rim_ref, fields_ref, table_ref, edge_ref, stack_ref
):
    blocks, members, node_cells = depth_ref.shape
    elements = node_cells // node_count
    face_rows = face_points * members
    stack_ref[...] = jnp.zeros_like(stack_ref)
    for pair in range(blocks // 2):
        lay_out(pair, (2 * pair, 2 * pair + 1), node_count, depth_ref, flow_ref, fields_ref)
        for face in range(faces):
            nodes = [int(node) for node in face_nodes[face][::-1]]
            stacked = stack_ref.at[pair % 2, face]
            for comp in range(3):
                stack_face(
                    fields_ref, pair, comp, nodes, members, node_count, stacked, comp * face_rows
                )
            turned = stacked[...].T
            for side in range(2):
                start = ((2 * pair + side) * faces + face) * elements
                table_ref[start : start + elements, :] = (
                    turned[side * elements : (side + 1) * elements]
                )

    def one_group(group, carry):
        for step in range(16):
            face = group * 16 + step
            edge_ref[pl.ds(face, 1), :] = table_ref[pl.ds(rim_ref[0, face], 1), :]
        return carry

    lax.fori_loop(0, rim_ref.shape[1] // 16, one_group, 0)


def section_kernel(
    face_nodes, node_count, members, low_start, early,
    order_ref, map_ref, rim_ref, wet_ref, breach_ref, chosen_ref, slot_ref, source_ref,
    depth_ref, flow_ref, metric_ref, scale_ref, angle_ref, links_ref, high_ref, low_ref,
    depth_out, flow_out,
    natural_ref, fields_ref, pool_ref, edge_ref, before_ref, after_ref, picked_ref, inner_ref,
    cos_ref, sin_ref, wall_ref, right_ref, moved_ref, send_ref, got_ref,
    rim_sems, send_sems, got_sems,
):
    blocks = depth_out.shape[0]
    elements = metric_ref.shape[2]
    lanes = 2 * elements
    rows = fields_ref.shape[2]
    full = members // 8 * 8
    rest = members - full
    face_rows = face_points * members
    halves = node_count // 2
    block_faces = faces * elements
    local_faces = blocks * block_faces
    rim = before_ref.shape[0]
    devices = got_ref.shape[0]
    own = lax.axis_index("mesh")
    mesh_type = pl.DeviceIdType.MESH

    barrier = pltpu.get_barrier_semaphore()
    for step in range(1, devices):
        pl.semaphore_signal(
            barrier, inc=1, device_id={"mesh": lax.rem(own + step, devices)},
            device_id_type=mesh_type,
        )

    make_table(
        face_nodes, node_count, depth_ref, flow_ref, rim_ref,
        natural_ref, pool_ref, edge_ref, inner_ref,
    )
    pl.semaphore_wait(barrier, devices - 1)

    to_next = pltpu.make_async_remote_copy(
        src_ref=edge_ref.at[pl.ds(rim, rim)], dst_ref=before_ref,
        send_sem=rim_sems.at[0], recv_sem=rim_sems.at[1],
        device_id={"mesh": lax.rem(own + 1, devices)}, device_id_type=mesh_type,
    )
    to_before = pltpu.make_async_remote_copy(
        src_ref=edge_ref.at[pl.ds(0, rim)], dst_ref=after_ref,
        send_sem=rim_sems.at[2], recv_sem=rim_sems.at[3],
        device_id={"mesh": lax.rem(own + devices - 1, devices)}, device_id_type=mesh_type,
    )

    @pl.when(own < devices - 1)
    def _():
        to_next.start()

    @pl.when(own > 0)
    def _():
        to_before.start()

    angles = angle_ref[...]
    cos_ref[...] = jnp.cos(angles)
    sin_ref[...] = jnp.sin(angles)
    own_number = (
        lax.broadcasted_iota(jnp.int32, angles.shape, 0) * block_faces
        + lax.broadcasted_iota(jnp.int32, angles.shape, 1)
    )
    wall_ref[...] = jnp.where(links_ref[...] == own_number, 1.0, 0.0)
    right_ref[...] = jnp.zeros_like(right_ref)
    filled = 3 * halves * members
    spare = moved_ref.shape[1] - filled
    if spare:
        moved_ref[:, filled:, :] = jnp.zeros((blocks, spare, lanes), jnp.float32)
    got_ref[own] = jnp.zeros(got_ref.shape[1:], jnp.float32)

    def volume(pair, right_ref):
        sides = (order_ref[2 * pair], order_ref[2 * pair + 1])
        lay_out(pair, sides, node_count, depth_ref, flow_ref, fields_ref)
        factors = jnp.concatenate([metric_ref[sides[0]], metric_ref[sides[1]]], axis=1)
        height = fields_ref[pair, 0]
        flow_x = fields_ref[pair, 1]
        flow_y = fields_ref[pair, 2]
        inverse = 1.0 / height
        pressure = 0.5 * gravity * height * height
        speed_x = flow_x * inverse
        speed_y = flow_y * inverse
        cross = flow_x * speed_y
        flux_f = (flow_x, flow_x * speed_x + pressure, cross)
        flux_g = (flow_y, cross, flow_y * speed_y + pressure)
        for comp in range(3):
            span = slice(comp * lanes, (comp + 1) * lanes)
            right_ref[0:rows, span] = factors[0:1] * flux_f[comp] + factors[2:3] * flux_g[comp]
            right_ref[rows : 2 * rows, span] = (
                factors[1:2] * flux_f[comp] + factors[3:4] * flux_g[comp]
            )

    for pair in range(early):
        volume(pair, right_ref.at[pair])

    @pl.when(own > 0)
    def _():
        to_next.wait_recv()
        pool_ref[local_faces : local_faces + rim, :] = before_ref[...]

    @pl.when(own < devices - 1)
    def _():
        to_before.wait_recv()
        pool_ref[local_faces + rim : local_faces + 2 * rim, :] = after_ref[...]

    def one_pair(pair, right_ref, picked_ref, inner_ref):
        sides = (order_ref[2 * pair], order_ref[2 * pair + 1])
        for side in range(2):
            for face in range(block_faces):
                picked_ref[side * block_faces + face : side * block_faces + face + 1, :] = pool_ref[
                    pl.ds(map_ref[sides[side], face], 1), :
                ]

        def face_row(ref, face):
            first = ref[pl.ds(sides[0], 1), :]
            second = ref[pl.ds(sides[1], 1), :]
            cells = slice(face * elements, (face + 1) * elements)
            return jnp.concatenate([first[:, cells], second[:, cells]], axis=1)

        for face in range(faces):
            nodes = [int(node) for node in face_nodes[face]]
            for comp in range(3):
                stack_face(
                    fields_ref, pair, comp, nodes, members, node_count,
                    inner_ref.at[face], comp * face_rows,
                )
            height = inner_ref[face, 0:face_rows]
            flow_x = inner_ref[face, face_rows : 2 * face_rows]
            flow_y = inner_ref[face, 2 * face_rows : 3 * face_rows]
            outside = jnp.concatenate(
                [
                    picked_ref[face * elements : (face + 1) * elements],
                    picked_ref[block_faces + face * elements : block_faces + (face + 1) * elements],
                ],
                axis=0,
            ).T
            normal_x = face_row(cos_ref, face)
            normal_y = face_row(sin_ref, face)
            wall = face_row(wall_ref, face) > 0.5
            half_scale = 0.5 * face_row(scale_ref, face)
            flow = flow_x * normal_x + flow_y * normal_y
            out_height = jnp.where(wall, height, outside[0:face_rows])
            out_x = jnp.where(
                wall, flow_x - 2.0 * flow * normal_x, outside[face_rows : 2 * face_rows]
            )
            out_y = jnp.where(
                wall, flow_y - 2.0 * flow * normal_y, outside[2 * face_rows : 3 * face_rows]
            )
            out_flow = out_x * normal_x + out_y * normal_y
            speed = flow / height
            out_speed = out_flow / out_height
            wave = jnp.maximum(
                jnp.abs(speed) + jnp.sqrt(gravity * height),
                jnp.abs(out_speed) + jnp.sqrt(gravity * out_height),
            )
            pressure = 0.5 * gravity * (height * height - out_height * out_height)
            jumps = (
                flow - out_flow + wave * (out_height - height),
                flow_x * speed - out_x * out_speed + pressure * normal_x + wave * (out_x - flow_x),
                flow_y * speed - out_y * out_speed + pressure * normal_y + wave * (out_y - flow_y),
            )
            start = 2 * rows + face * face_rows
            for comp in range(3):
                right_ref[start : start + face_rows, comp * lanes : (comp + 1) * lanes] = (
                    half_scale * jumps[comp]
                )

        right = right_ref[...]
        right_high = right.astype(jnp.bfloat16)
        right_low = (right - right_high.astype(jnp.float32)).astype(jnp.bfloat16)
        high = high_ref[...]
        tendency = (
            jnp.dot(high, right_high, preferred_element_type=jnp.float32)
            + jnp.dot(high, right_low, preferred_element_type=jnp.float32)
            + jnp.dot(
                low_ref[...], right_high[low_start:], preferred_element_type=jnp.float32
            )
        )
        row_low = lanes_low((1, lanes), elements)
        step = time_step * jnp.where(
            row_low, wet_ref[sides[0]].astype(jnp.float32), wet_ref[sides[1]].astype(jnp.float32)
        )

        def inflow(member):
            return breach_rate * jnp.where(
                row_low,
                breach_ref[member, sides[0]].astype(jnp.float32),
                breach_ref[member, sides[1]].astype(jnp.float32),
            )

        def inflow_rows(first, size):
            row_ids = lax.broadcasted_iota(jnp.int32, (size, lanes), 0)
            total = jnp.zeros((size, lanes), jnp.float32)
            for member in range(size):
                total = jnp.where(row_ids == member, inflow(first + member), total)
            return total

        for first, size in ((0, full), (full, rest)):
            source = inflow_rows(first, size)
            low = lanes_low((size, lanes), elements)
            for comp in range(3):
                span = slice(comp * lanes, (comp + 1) * lanes)
                for half in range(node_count // 2):
                    both = []
                    for side in range(2):
                        base = node_count * first + (2 * half + side) * size
                        change = tendency[base : base + size, span]
                        if comp == 0:
                            change = change + source
                        both.append(fields_ref[pair, comp, base : base + size, :] + step * change)
                    one = jnp.where(low, both[0], pltpu.roll(both[1], elements, 1))
                    two = jnp.where(low, pltpu.roll(both[0], elements, 1), both[1])
                    base = halves * 3 * first + (comp * halves + half) * size
                    moved_ref[2 * pair, base : base + size, :] = one
                    moved_ref[2 * pair + 1, base : base + size, :] = two


    def late_pair(pair, carry):
        volume(pair, right_ref.at[0])
        one_pair(pair, right_ref.at[0], picked_ref.at[0], inner_ref.at[0])
        return carry

    for pair in range(early):
        one_pair(pair, right_ref.at[pair], picked_ref.at[pair % 2], inner_ref.at[pair % 2])

    def one_send(device, carry):
        send_ref[device] = moved_ref[chosen_ref[device]]
        return carry

    lax.fori_loop(0, devices, one_send, 0, unroll=4)
    sends = []
    half_devices = devices // 2
    own_half = own // half_devices
    for step in [*range(half_devices, devices), *range(1, half_devices)]:
        side = own_half if step < half_devices else 1 - own_half
        target = side * half_devices + lax.rem(own + step, half_devices)
        sends.append(
            pltpu.make_async_remote_copy(
                src_ref=send_ref.at[target], dst_ref=got_ref.at[own],
                send_sem=send_sems.at[target], recv_sem=got_sems.at[own],
                device_id={"mesh": target}, device_id_type=mesh_type,
            )
        )
    for copy in sends:
        copy.start()

    lax.fori_loop(early, blocks // 2, late_pair, 0)

    for step in range(1, devices):
        origin = lax.rem(own + step, devices)
        pltpu.make_async_remote_copy(
            src_ref=send_ref.at[origin], dst_ref=got_ref.at[origin],
            send_sem=send_sems.at[origin], recv_sem=got_sems.at[origin],
            device_id={"mesh": origin}, device_id_type=mesh_type,
        ).wait_recv()

    def one_slot(slot, carry):
        stays = source_ref[slot] == own
        block = jnp.where(stays, moved_ref[slot_ref[slot]], got_ref[source_ref[slot]])
        for comp in range(3):
            for half in range(halves):
                for first, size in ((0, full), (full, rest)):
                    base = halves * 3 * first + (comp * halves + half) * size
                    value = block[base : base + size]
                    cells = (slice(first, first + size), slice(half * lanes, (half + 1) * lanes))
                    if comp == 0:
                        depth_out[(slot, *cells)] = value
                    else:
                        flow_out[(slot, comp - 1, *cells)] = value
        return carry

    lax.fori_loop(0, blocks, one_slot, 0, unroll=4)
    for copy in sends:
        copy.wait_send()

    @pl.when(own < devices - 1)
    def _():
        to_next.wait_send()

    @pl.when(own > 0)
    def _():
        to_before.wait_send()


def body(
    water_depth,
    momentum,
    metric,
    face_scale,
    face_angle,
    face_map,
    rim_faces,
    wet_blocks,
    breach,
    block_plan,
):
    face_nodes = node_tables()[3]
    node_count = int(face_nodes.max()) + 1
    blocks, members, node_cells = water_depth.shape
    elements = node_cells // node_count
    lanes = 2 * elements
    rows = round_up(node_count * members, 16)
    block_faces = faces * elements
    local_faces = blocks * block_faces
    rim_count = rim_faces.shape[1]
    rim = rim_count // 2
    own = lax.axis_index("mesh").astype(jnp.int32)
    devices = lax.axis_size("mesh")
    f32 = jnp.float32

    local_ids = jnp.arange(blocks, dtype=jnp.int32)
    slot_ids = own * blocks + local_ids
    every_slot = jnp.arange(block_plan.shape[0], dtype=jnp.int32)
    targets = jnp.sum(
        jnp.where(every_slot[None, :] == slot_ids[:, None], block_plan[None, :], 0), axis=1
    ) // blocks
    stays = (targets == own).astype(jnp.int32)
    keys = stays * blocks + local_ids
    place = jnp.sum((keys[None, :] < keys[:, None]).astype(jnp.int32), axis=1)
    order = jnp.sum(jnp.where(place[None, :] == local_ids[:, None], local_ids[None, :], 0), axis=1)
    device_ids = jnp.arange(devices, dtype=jnp.int32)
    chosen = jnp.sum(jnp.where(targets[None, :] == device_ids[:, None], place[None, :], 0), axis=1)
    chosen = jnp.where(device_ids == own, 0, chosen)
    source = jnp.sum(
        jnp.where(block_plan[None, :] == slot_ids[:, None], every_slot[None, :], 0), axis=1
    )
    origin = jnp.clip(source - own * blocks, 0, blocks - 1)
    slot_place = jnp.sum(jnp.where(origin[:, None] == local_ids[None, :], place[None, :], 0), axis=1)
    source = source // blocks

    high, low = combined_matrix(members, rows, node_count)
    low_start = 2 * rows if not np.any(low[:, : 2 * rows].astype(np.float32)) else 0
    early = min(-(-(devices // 2) // 2), blocks // 2)
    block_rows = round_up(3 * members * (node_count // 2), 8)
    return pl.pallas_call(
        lambda *refs: section_kernel(face_nodes, node_count, members, low_start, early, *refs),
        out_shape=(
            jax.ShapeDtypeStruct(water_depth.shape, f32),
            jax.ShapeDtypeStruct(momentum.shape, f32),
        ),
        in_specs=[SMEM] * 8 + [VMEM] * 8,
        out_specs=(VMEM, VMEM),
        scratch_shapes=[
            pltpu.VMEM((blocks // 2, 3, rows, lanes), f32),
            pltpu.VMEM((blocks // 2, 3, rows, lanes), f32),
            pltpu.VMEM((local_faces + rim_count, lanes), f32),
            pltpu.VMEM((rim_count, lanes), f32),
            pltpu.VMEM((rim, lanes), f32),
            pltpu.VMEM((rim, lanes), f32),
            pltpu.VMEM((2, 2 * block_faces, lanes), f32),
            pltpu.VMEM((2, faces, lanes, lanes), f32),
            pltpu.VMEM((blocks, block_faces), f32),
            pltpu.VMEM((blocks, block_faces), f32),
            pltpu.VMEM((blocks, block_faces), f32),
            pltpu.VMEM((early, high.shape[1], 3 * lanes), f32),
            pltpu.VMEM((blocks, block_rows, lanes), f32),
            pltpu.VMEM((devices, block_rows, lanes), f32),
            pltpu.VMEM((devices, block_rows, lanes), f32),
            pltpu.SemaphoreType.DMA((4,)),
            pltpu.SemaphoreType.DMA((devices,)),
            pltpu.SemaphoreType.DMA((devices,)),
        ],
        compiler_params=pltpu.CompilerParams(
            vmem_limit_bytes=48 * 2**20, collective_id=0, has_side_effects=True
        ),
    )(
        order, face_map, rim_faces, wet_blocks, breach.T, chosen,
        slot_place, source, water_depth, momentum, metric, face_scale, face_angle, face_map,
        jnp.asarray(high), jnp.asarray(low[:, low_start:]),
    )


def solution(mesh):
    in_specs = (
        P(("groups", "mesh"), None, None),
        P(("groups", "mesh"), None, None, None),
        P(("groups", "mesh"), None, None),
        P(("groups", "mesh"), None),
        P(("groups", "mesh"), None),
        P(("groups", "mesh"), None),
        P(("groups", "mesh"), None),
        P(("groups", "mesh")),
        P(("groups", "mesh"), None),
        P("groups"),
    )
    out_specs = (P(("groups", "mesh"), None, None), P(("groups", "mesh"), None, None, None))
    return jax.shard_map(body, mesh=mesh, in_specs=in_specs, out_specs=out_specs, check_vma=False)
```
